512 devices in a mesh: expert: 16 (over y, core), tensor: 8 (over z), dp: 4 (over x).
Axes of the slice: x: 4, y: 8, z: 8, core: 2. Of those that a mesh axis runs over, the one named last changes fastest.
Arguments:
- enc_tokens: bfloat16 [2048, 2048], P('expert', ('tensor', 'dp')), may hold values from -6 to 6
- enc_experts: int32 [2048, 2], P('expert'), may hold values from 0 to 15, all different within a row; in each aligned block of 128 rows (0 to 127, 128 to 255, ...) at most 32 rows name the same one
- enc_levels: int32 [2048, 2], P('expert'), may hold values from 1 to 255
- enc_w_in: bfloat16 [16, 2048, 8192], P('expert', None, ('tensor', 'dp')), may hold values from -0.125 to 0.125
- enc_w_out: bfloat16 [16, 8192, 2048], P('expert', ('tensor', 'dp')), may hold values from -0.125 to 0.125
- dec_tokens: bfloat16 [2304, 2048], P('expert', ('tensor', 'dp')), may hold values from -6 to 6
- dec_lengths: int32 [16, 16], P('expert'), may hold values from 1 to 16, as said below
- dec_language: int32 [256, 1], P('expert'), may hold values from 0 to 15, as said below
- dec_w_in: bfloat16 [16, 2048, 8192], P('expert', None, ('tensor', 'dp')), may hold values from -0.125 to 0.125
- dec_w_out: bfloat16 [16, 8192, 2048], P('expert', ('tensor', 'dp')), may hold values from -0.125 to 0.125
Outputs:
- enc_mixed: bfloat16 [2048, 2048], P('expert', ('tensor', 'dp'))
- dec_mixed: bfloat16 [2304, 2048], P('expert', ('tensor', 'dp'))
The draws below stay inside these ranges and needn't reach their ends.
Inputs may be any that keep to these rules, and one draw needn't show every extreme that they name: `enc_experts`: the two experts of a token differ. Among the 256 assignments of one token group (aligned blocks of 128 rows), at most 32 name one expert, and in every draw some group gives some expert exactly 32. `dec_lengths`: each row sums to 144; exactly two entries of each row equal 16. `dec_language`: at most two of the 16 sentences of one token group (aligned blocks of 16 rows) go to one expert, so at most 32 of a group's decoder tokens reach one expert; in every draw some group sends exactly 32 tokens to one expert.
All inputs are finite; a program needn't handle non-finite values.
Results may differ from the reference program's by a relative error of at most 0.015.
Values may be sent and summed in bfloat16 or wider, within the bound.
No kernel may reach another device: no remote copies, remote signals or barrier semaphores. Data moves between devices by JAX's collectives and lax.ppermute only.
A program may use at most 64 MiB of HBM per device.

```python
import math
import jax
import jax.numpy as jnp
import numpy as np
from jax import lax

D = 2048
FF = 8192
TOK_DEV = 128
EXPERTS = 16
SENTS = 16
GROUPS = 16
BLOCKS = 32
CAP_ENC = 32
LEN_MAX = 16
DEC_DEV = 144
CAP_DEC = 32
TOKENS = 2048
DEC_TOKENS = 2304
SENTENCES = 256


def sentence_layout(key):
    key_pairs, key_order, key_spread, key_paired, key_special = jax.random.split(key, 5)
    pair_count = (SENTS - 2) // 2
    shorter = jax.random.randint(key_pairs, (GROUPS, pair_count), 1, LEN_MAX, dtype=jnp.int32)
    base_lengths = jnp.concatenate([shorter, LEN_MAX - shorter, jnp.full((GROUPS, 2), LEN_MAX, jnp.int32)], axis=1)
    doubled = jnp.arange(2 * EXPERTS, dtype=jnp.int32) // 2
    spread_keys = jax.random.split(key_spread, GROUPS)
    spread = jax.vmap(lambda k: jax.random.permutation(k, doubled)[:SENTS])(spread_keys)
    paired_keys = jax.random.split(key_paired, GROUPS)
    paired_experts = jax.vmap(lambda k: jax.random.permutation(k, jnp.arange(EXPERTS, dtype=jnp.int32))[:SENTS // 2])(paired_keys)
    paired = jnp.repeat(paired_experts, 2, axis=1)
    special = jax.random.randint(key_special, (), 0, GROUPS, dtype=jnp.int32)
    is_special = (jnp.arange(GROUPS, dtype=jnp.int32) == special)[:, None]
    base_language = jnp.where(is_special, paired, spread)
    order_keys = jax.random.split(key_order, GROUPS)
    order = jax.vmap(lambda k: jax.random.permutation(k, jnp.arange(SENTS, dtype=jnp.int32)))(order_keys)
    lengths = jnp.take_along_axis(base_lengths, order, axis=1).astype(jnp.int32)
    language = jnp.take_along_axis(base_language, order, axis=1).astype(jnp.int32)
    return (lengths, language)


def draw_dec_lengths(key, part):
    lengths, language = sentence_layout(key)
    return lengths


def draw_dec_language(key, part):
    lengths, language = sentence_layout(key)
    return language.reshape(SENTENCES, 1)


def plant(values, rng, least, largest):
    longest = values.shape.index(max(values.shape))
    spots = []
    for shift in (0, 1):
        where = [jax.random.randint(jax.random.fold_in(rng, axis), (), 0, length) for axis, length in enumerate(values.shape)]
        where[longest] = (where[longest] + shift) % values.shape[longest]
        spots.append(tuple(where))
    return values.at[spots[0]].set(least).at[spots[1]].set(largest)


def strengthened(result, key, source, target, shards_of, factor):
    owner, partner = [(jnp.arange(result.shape[axis_at]) // (result.shape[axis_at] // shards_of)).reshape([-1 if axis == axis_at else 1 for axis in range(result.ndim)]) for axis_at in (source, target)]
    chosen = jax.random.permutation(key, shards_of)[partner]
    strong = (owner == chosen) | (owner == (partner + shards_of // 2) % shards_of)
    return jnp.where(strong, factor * result, result)


def level_of(rng, dims, pieces, smallest, high):
    def one(axis_at, blocks):
        steps = jax.random.uniform(jax.random.fold_in(jax.random.fold_in(rng, 6), axis_at), (blocks,), jnp.float32, smallest / len(pieces), high / len(pieces))
        return jnp.repeat(jnp.exp(steps), dims[axis_at] // blocks).reshape((-1,) + (1,) * (len(dims) - axis_at - 1))

    level = one(*pieces[0])
    for cut in pieces[1:]:
        level = level * one(*cut)
    return level


def shared_out(rng, own, number, rows, number_of, top, bound, slope):
    order = jax.random.permutation(rng, number_of)
    heavy_load, ordinary = shares(number_of, rows * top, bound, slope, True), shares(number_of, rows * top, bound, slope, False)
    places = jnp.arange(number_of)

    def named(sizes, offset_by):
        used = int((sizes > 0).sum())
        fixed = max(1, used // 4)
        shifted = fixed + (places - fixed + offset_by * (used - fixed)) % max(1, number_of - fixed)
        return jnp.zeros((number_of,), jnp.int32).at[order[jnp.where(places < fixed, places, shifted)]].set(jnp.asarray(sizes, jnp.int32))

    sizes = jnp.where(number % 4 == 0, named(heavy_load, number // 4), named(ordinary, number - number // 4 - 1))
    mixed = jax.random.permutation(jax.random.fold_in(own, 3), number_of)
    donor, sink = mixed[0:number_of // 2 * 2:2], mixed[1:number_of // 2 * 2:2]
    slack = jnp.minimum(sizes[donor] - 1, bound - sizes[sink]) // 2
    slack = jnp.where((donor == order[0]) | (sink == order[0]) | (sizes[sink] == 0), 0, jnp.maximum(slack, 0))
    shifted = jax.random.randint(jax.random.fold_in(own, 4), (number_of // 2,), 0, 1 << 20) % (slack + 1)
    sizes = sizes.at[donor].add(-shifted).at[sink].add(shifted)
    items = jnp.searchsorted(jnp.cumsum(sizes), jnp.arange(rows * top), side="right").astype(jnp.int32)
    table = items.reshape(top, rows).T
    table = table[jax.random.permutation(jax.random.fold_in(own, 1), rows)]
    offset_by = jax.random.randint(jax.random.fold_in(own, 2), (rows, 1), 0, top)
    return jnp.take_along_axis(table, (jnp.arange(top)[None, :] + offset_by) % top, axis=1)


def shares(amount, total, bound, skew, full):
    weights = [(1 << 20) // math.isqrt(grade ** skew) + 1 for grade in range(1, amount + 1)]
    largest = bound if full else min(bound, max(-(-total // amount), total * weights[0] // sum(weights)))
    least = 1 if total - largest >= amount - 1 else 0
    given, rest = [largest] + [least] * (amount - 1), total - largest - least * (amount - 1)
    while rest > 0:
        candidates = [i for i in range(1, amount) if given[i] < largest] or [i for i in range(1, amount) if given[i] < bound]
        mass, left = sum([weights[i] for i in candidates]), rest
        for i in candidates:
            more = min(bound - given[i], max(1, left * weights[i] // mass), rest)
            given[i] = given[i] + more
            rest = rest - more
    return np.array(given)


def noise(own_key, shape, width, most, cuts=(), kind=jnp.bfloat16):
    level = level_of(own_key, shape, cuts, -0.22, 0.18) if cuts else 1.0
    result = jax.random.normal(own_key, shape, jnp.float32) * width * level
    return jnp.minimum(jnp.maximum(result, -most), most).astype(kind)


def gaussian_with(key, shape, scale, bound, cuts, heavy, held_as=jnp.bfloat16):
    entries = scale * jax.random.normal(key, shape, jnp.float32)
    if cuts:
        entries = entries * level_of(key, shape, cuts, -0.22, 0.18)
    return jnp.clip(strengthened(entries, jax.random.fold_in(key, 3), *heavy), -bound, bound).astype(held_as)


def setup_inputs(seed: int = 0) -> dict:
    keys = jax.random.split(jax.random.key(seed), 11)
    enc_tokens = noise(keys[0], (TOKENS, D), 1.0, 6.0, ((0, 16), (1, 32)))
    enc_experts_keys = jax.random.split(jax.random.fold_in(keys[1], 1), TOKENS // TOK_DEV)
    enc_experts_turns = jax.random.permutation(jax.random.fold_in(keys[1], 3), TOKENS // TOK_DEV)
    enc_experts = jax.vmap(lambda own, number: shared_out(jax.random.fold_in(keys[1], 2), own, number, TOK_DEV, EXPERTS, 2, CAP_ENC, 1))(enc_experts_keys, enc_experts_turns).reshape((TOKENS, 2))
    enc_levels = plant(jax.random.randint(keys[2], (TOKENS, 2), 1, 256), jax.random.fold_in(keys[2], 1), 1, 255).astype(jnp.int32)
    enc_w_in = noise(keys[3], (EXPERTS, D, FF), D ** -0.5, 0.125, ((0, 16), (2, 32)))
    enc_w_out = gaussian_with(keys[4], (EXPERTS, FF, D), FF ** -0.5, 0.125, ((0, 16), (1, 32)), (1, 2, 32, 2.75))
    dec_tokens = noise(keys[5], (DEC_TOKENS, D), 1.0, 6.0, ((0, 16), (1, 32)))
    dec_lengths = draw_dec_lengths(jax.random.fold_in(keys[10], 71), 0)
    dec_language = draw_dec_language(jax.random.fold_in(keys[10], 71), 0)
    dec_w_in = noise(keys[8], (EXPERTS, D, FF), D ** -0.5, 0.125, ((0, 16), (2, 32)))
    dec_w_out = gaussian_with(keys[9], (EXPERTS, FF, D), FF ** -0.5, 0.125, ((0, 16), (1, 32)), (1, 2, 32, 2.75))
    return {"enc_tokens": enc_tokens, "enc_experts": enc_experts, "enc_levels": enc_levels, "enc_w_in": enc_w_in, "enc_w_out": enc_w_out, "dec_tokens": dec_tokens, "dec_lengths": dec_lengths, "dec_language": dec_language, "dec_w_in": dec_w_in, "dec_w_out": dec_w_out}


def expert_outputs(buffers, weight_in, weight_out):
    unit_count = FF // BLOCKS

    def one_expert(operands):
        row_block, first_matrix, second_matrix = operands
        parts_in = first_matrix.reshape(D, BLOCKS, unit_count)
        parts_out = second_matrix.reshape(BLOCKS, unit_count, D)

        def one_block(total, index):
            columns = lax.dynamic_index_in_dim(parts_in, index, 1, keepdims=False)
            hidden = jax.nn.relu(jnp.dot(row_block, columns, preferred_element_type=jnp.float32)).astype(jnp.bfloat16)
            lines = lax.dynamic_index_in_dim(parts_out, index, 0, keepdims=False)
            partial_value = jnp.dot(hidden, lines, preferred_element_type=jnp.float32).astype(jnp.bfloat16)
            partial_value = lax.optimization_barrier(partial_value)
            return total + partial_value.astype(jnp.float32), None

        start_total = jnp.zeros((row_block.shape[0], D), jnp.float32)
        summed, _ = lax.scan(one_block, start_total, jnp.arange(BLOCKS, dtype=jnp.int32))
        return lax.optimization_barrier(summed.astype(jnp.bfloat16))

    return lax.map(one_expert, (buffers, weight_in, weight_out))


def reference(enc_tokens, enc_experts, enc_levels, enc_w_in, enc_w_out, dec_tokens, dec_lengths, dec_language, dec_w_in, dec_w_out):
    grouped = enc_experts.reshape(GROUPS, 2 * TOK_DEV)
    onehot = (grouped[:, :, None] == jnp.arange(EXPERTS, dtype=jnp.int32)[None, None, :]).astype(jnp.int32)
    earlier = jnp.cumsum(onehot, axis=1) - onehot
    enc_slot = jnp.sum(earlier * onehot, axis=2).astype(jnp.int32)
    group_index = jnp.arange(GROUPS, dtype=jnp.int32)[:, None]
    enc_rows = (group_index * CAP_ENC + enc_slot).reshape(-1).astype(jnp.int32)
    enc_ids = enc_experts.reshape(-1).astype(jnp.int32)
    repeated = jnp.repeat(enc_tokens, 2, axis=0)
    enc_buffer = jnp.zeros((EXPERTS, GROUPS * CAP_ENC, D), jnp.bfloat16).at[enc_ids, enc_rows].set(repeated)
    enc_result = expert_outputs(enc_buffer, enc_w_in, enc_w_out)
    picked = enc_result[enc_ids, enc_rows].astype(jnp.float32).reshape(TOKENS, 2, D)
    levels = enc_levels.astype(jnp.float32)
    gate = levels / jnp.sum(levels, axis=1, keepdims=True)
    enc_mixed = enc_tokens.astype(jnp.float32) + gate[:, 0:1] * picked[:, 0, :] + gate[:, 1:2] * picked[:, 1, :]

    sentence_ends = jnp.cumsum(dec_lengths, axis=1).astype(jnp.int32)
    places = jnp.arange(DEC_DEV, dtype=jnp.int32)
    sentence = jnp.sum((places[None, :, None] >= sentence_ends[:, None, :]).astype(jnp.int32), axis=2).astype(jnp.int32)
    languages = dec_language.reshape(GROUPS, SENTS)
    target_grid = jnp.take_along_axis(languages, sentence, axis=1).astype(jnp.int32)
    dec_onehot = (target_grid[:, :, None] == jnp.arange(EXPERTS, dtype=jnp.int32)[None, None, :]).astype(jnp.int32)
    dec_earlier = jnp.cumsum(dec_onehot, axis=1) - dec_onehot
    dec_slot = jnp.sum(dec_earlier * dec_onehot, axis=2).astype(jnp.int32)
    dec_target = target_grid.reshape(-1).astype(jnp.int32)
    dec_rows = (group_index * CAP_DEC + dec_slot).reshape(-1).astype(jnp.int32)
    dec_buffer = jnp.zeros((EXPERTS, GROUPS * CAP_DEC, D), jnp.bfloat16).at[dec_target, dec_rows].set(dec_tokens)
    dec_result = expert_outputs(dec_buffer, dec_w_in, dec_w_out)
    dec_mixed = dec_tokens.astype(jnp.float32) + dec_result[dec_target, dec_rows].astype(jnp.float32)
    return enc_mixed.astype(jnp.bfloat16), dec_mixed.astype(jnp.bfloat16)
```

```python
import jax
import jax.numpy as jnp
from jax import lax
from jax.experimental import pallas as pl
from jax.experimental.pallas import tpu as pltpu
from jax.sharding import PartitionSpec as P

BF = jnp.bfloat16
F32 = jnp.float32
EXPERTS = 16
CAP = 32
ROWS = EXPERTS * CAP
FEATS = 64
T = 8
DP = 4
UNITS = 256
VMEM = pl.BlockSpec(memory_space=pltpu.VMEM)
SMEM = pl.BlockSpec(memory_space=pltpu.SMEM)


def call(body, out_shape, n_in, *, smem=(), flops=0, moved=0):
    many = isinstance(out_shape, (tuple, list))
    return pl.pallas_call(
        body,
        out_shape=out_shape,
        in_specs=[SMEM if i in smem else VMEM for i in range(n_in)],
        out_specs=[VMEM] * len(out_shape) if many else VMEM,
        compiler_params=pltpu.CompilerParams(vmem_limit_bytes=32 * 1024 * 1024),
        cost_estimate=pl.CostEstimate(flops=flops, bytes_accessed=moved, transcendentals=0),
    )


def shape(dims, dtype=BF):
    return jax.ShapeDtypeStruct(dims, dtype)


def nt(a, b):
    return lax.dot_general(a, b, (((1,), (1,)), ((), ())), preferred_element_type=F32)


def nn(a, b):
    return lax.dot_general(a, b, (((1,), (0,)), ((), ())), preferred_element_type=F32)


def iota(dims, axis):
    return lax.broadcasted_iota(jnp.int32, dims, axis)


def pick(target):
    span = target.shape[1]
    return (iota((ROWS, span), 0) == target).astype(F32).astype(BF)


def slots(onehots):
    total = sum(onehots)
    span = total.shape[1]
    before = (iota((span, span), 0) < iota((span, span), 1)).astype(F32).astype(BF)
    earlier = nn(total.astype(BF), before)
    return [jnp.sum(o * earlier, axis=0, keepdims=True).astype(jnp.int32) for o in onehots]


def place_body(experts, lengths, languages, enc, dec, sent, enc_at, dec_at):
    enc_count = enc.shape[1]
    dec_count = dec.shape[1]
    rank = iota((EXPERTS, enc_count), 0)
    named = [experts[k : k + 1, :] for k in range(2)]
    found = slots([(rank == e).astype(F32) for e in named])
    targets = [e * CAP + s for e, s in zip(named, found)]
    for k in range(2):
        enc_at[k : k + 1, :] = targets[k]

    sents = lengths.shape[1]
    square = (sents, sents)
    upto = iota(square, 1) <= iota(square, 0)
    same = iota(square, 1) == iota(square, 0)
    length = jnp.broadcast_to(lengths[...], square)
    language = jnp.broadcast_to(languages[...], square)
    ends = jnp.sum(jnp.where(upto, length, 0), axis=1, keepdims=True)
    begins = ends - jnp.sum(jnp.where(same, length, 0), axis=1, keepdims=True)
    spoken = jnp.sum(jnp.where(same, language, 0), axis=1, keepdims=True)
    places = iota((sents, dec_count), 1)
    member = (places >= begins) & (places < ends)
    chosen = jnp.sum(jnp.where(member, spoken, 0), axis=0, keepdims=True)
    (dec_slot,) = slots([(iota((EXPERTS, dec_count), 0) == chosen).astype(F32)])
    dec_target = chosen * CAP + dec_slot
    dec_at[...] = dec_target

    zeros_enc = jnp.zeros((FEATS, enc_count), BF)
    zeros_dec = jnp.zeros((FEATS, dec_count), BF)
    wide_enc = jnp.concatenate([enc[...], zeros_enc], axis=0)
    wide_dec = jnp.concatenate([zeros_dec, dec[...]], axis=0)
    enc_pick = pick(targets[0]) + pick(targets[1])
    rows = nt(enc_pick, wide_enc) + nt(pick(dec_target), wide_dec)
    sent[...] = rows.astype(BF).reshape(EXPERTS, CAP, 2 * FEATS)


def spread_body(got, enc, dec):
    turned = got[...].reshape(ROWS, 2 * FEATS).astype(F32).T.astype(BF)
    for t in range(T):
        enc[t] = turned[:FEATS]
        dec[t] = turned[FEATS:]


def turn_body(w_in, w_out, in_turned, out_turned):
    for d in range(DP):
        cut = [(t * DP + d) * FEATS for t in range(T)]
        block = jnp.concatenate([w_in[c : c + FEATS, :] for c in cut], axis=0)
        in_turned[d] = block.T
    for c in range(16):
        turned = w_out[:, c * 128 : (c + 1) * 128].T
        for half in range(2):
            b = c * 2 + half
            t, d = b // DP, b % DP
            out_turned[d, t * FEATS : (t + 1) * FEATS, :] = turned[half * FEATS : (half + 1) * FEATS]


def expert_body(me, x0, x1, x2, x3, w_in, w_out, p0, p1, p2, p3):
    d = me[0]
    hidden = None
    for k, x in enumerate((x0, x1, x2, x3)):
        source = lax.rem(d - k + DP, DP)
        term = nn(w_in[source], x[...])
        hidden = term if hidden is None else hidden + term
    hidden = jnp.maximum(hidden, 0.0).astype(BF)
    for k, p in enumerate((p0, p1, p2, p3)):
        goal = lax.rem(d + k, DP)
        p[...] = nn(w_out[goal], hidden).astype(BF)


def add_body(a, b, c, d, out):
    total = (a[...].astype(F32) + b[...].astype(F32)) + (c[...].astype(F32) + d[...].astype(F32))
    out[...] = total.astype(BF)


def pack_body(enc, dec, sent):
    def total(ref):
        acc = ref[0].astype(F32)
        for t in range(1, T):
            acc = acc + ref[t].astype(F32)
        return acc.astype(BF).astype(F32)

    both = jnp.concatenate([total(enc), total(dec)], axis=0)
    sent[...] = both.T.astype(BF).reshape(EXPERTS, CAP, 2 * FEATS)


def mix_body(got, enc_at, dec_at, levels, enc, dec, enc_out, dec_out):
    turned = got[...].reshape(ROWS, 2 * FEATS).astype(F32).T.astype(BF)
    level = levels[...].astype(F32)
    whole = level[0:1] + level[1:2]
    mixed = enc[...].astype(F32)
    for k in range(2):
        rows = nn(turned[:FEATS], pick(enc_at[k : k + 1, :]))
        mixed = mixed + (level[k : k + 1] / whole) * rows
    enc_out[...] = mixed.astype(BF)
    rows = nn(turned[FEATS:], pick(dec_at[...]))
    dec_out[...] = (dec[...].astype(F32) + rows).astype(BF)


def shift(value, k):
    return lax.ppermute(value, "dp", [(i, (i + k) % DP) for i in range(DP)])


def gather(block, turned, me):
    over_t = lax.all_to_all(block, "tensor", split_axis=0, concat_axis=0, tiled=True)
    own = over_t.reshape(T * FEATS, ROWS)
    return [own] + [shift(own, k) for k in (1, 2, 3)]


def expert(blocks, turned, me):
    part = shape((T * FEATS, ROWS))
    work = 4 * ROWS * UNITS * T * DP * FEATS
    return call(expert_body, [part] * 4, 7, smem=(0,), flops=work, moved=6 << 20)(me, *blocks, *turned)


def scatter(parts):
    sums = [parts[0]] + [shift(parts[k], k) for k in (1, 2, 3)]
    total = call(add_body, shape((T * FEATS, ROWS)), 4, moved=5 << 19)(*sums)
    total = total.reshape(T, FEATS, ROWS)
    return lax.all_to_all(total, "tensor", split_axis=0, concat_axis=0, tiled=True)


def shards(
    enc_tokens,
    enc_experts,
    enc_levels,
    enc_w_in,
    enc_w_out,
    dec_tokens,
    dec_lengths,
    dec_language,
    dec_w_in,
    dec_w_out,
):
    me = lax.axis_index("dp").astype(jnp.int32).reshape(1)
    enc = enc_tokens.T
    dec = dec_tokens.T
    packed = shape((EXPERTS, CAP, 2 * FEATS))
    sent, enc_at, dec_at = call(
        place_body,
        [packed, shape((2, enc.shape[1]), jnp.int32), shape((1, dec.shape[1]), jnp.int32)],
        5,
        moved=1 << 18,
    )(enc_experts.T, dec_lengths, dec_language.T, enc, dec)
    got = lax.all_to_all(sent, "expert", split_axis=0, concat_axis=0, tiled=True)

    def turn(w_in, w_out):
        out = [shape((DP, UNITS, T * FEATS)), shape((DP, T * FEATS, UNITS))]
        return call(turn_body, out, 2, moved=4 << 20)(w_in[0], w_out[0])

    enc_turned = turn(enc_w_in, enc_w_out)
    dec_turned = turn(dec_w_in, dec_w_out)
    block = shape((T, FEATS, ROWS))
    enc_block, dec_block = call(spread_body, [block, block], 1, moved=1 << 20)(got)

    enc_x = gather(enc_block, enc_turned, me)
    dec_x = gather(dec_block, dec_turned, me)
    enc_sums = scatter(expert(enc_x, enc_turned, me))
    dec_sums = scatter(expert(dec_x, dec_turned, me))

    back = call(pack_body, packed, 2, moved=1 << 20)(enc_sums, dec_sums)
    got = lax.all_to_all(back, "expert", split_axis=0, concat_axis=0, tiled=True)
    enc_out, dec_out = call(
        mix_body, [shape(enc.shape), shape(dec.shape)], 6, moved=1 << 18
    )(got, enc_at, dec_at, enc_levels.T, enc, dec)
    return enc_out.T, dec_out.T


def solution(mesh):
    return jax.shard_map(
        shards,
        mesh=mesh,
        in_specs=(
            P("expert", ("tensor", "dp")),
            P("expert", None),
            P("expert", None),
            P("expert", None, ("tensor", "dp")),
            P("expert", ("tensor", "dp"), None),
            P("expert", ("tensor", "dp")),
            P("expert", None),
            P("expert", None),
            P("expert", None, ("tensor", "dp")),
            P("expert", ("tensor", "dp"), None),
        ),
        out_specs=(P("expert", ("tensor", "dp")), P("expert", ("tensor", "dp"))),
        check_vma=False,
    )
```

```python
import jax
import jax.numpy as jnp
from jax import lax
from jax.experimental import pallas as pl
from jax.experimental.pallas import tpu as pltpu
from jax.sharding import PartitionSpec as P

BF = jnp.bfloat16
F32 = jnp.float32
EXPERTS = 16
CAP = 32
ROWS = EXPERTS * CAP
FEATS = 64
HELD = 256
LINES = CAP + 16
T = 8
DP = 4
UNITS = 256
VMEM = pl.BlockSpec(memory_space=pltpu.VMEM)
SMEM = pl.BlockSpec(memory_space=pltpu.SMEM)


def call(body, out_shape, n_in, *, smem=(), smem_out=(), flops=0, moved=0):
    many = isinstance(out_shape, (tuple, list))
    outs = [SMEM if i in smem_out else VMEM for i in range(len(out_shape))] if many else VMEM
    return pl.pallas_call(
        body,
        out_shape=out_shape,
        in_specs=[SMEM if i in smem else VMEM for i in range(n_in)],
        out_specs=outs,
        compiler_params=pltpu.CompilerParams(vmem_limit_bytes=32 * 1024 * 1024),
        cost_estimate=pl.CostEstimate(flops=flops, bytes_accessed=moved, transcendentals=0),
    )


def shape(dims, dtype=BF):
    return jax.ShapeDtypeStruct(dims, dtype)


def nt(a, b):
    return lax.dot_general(a, b, (((1,), (1,)), ((), ())), preferred_element_type=F32)


def nn(a, b):
    return lax.dot_general(a, b, (((1,), (0,)), ((), ())), preferred_element_type=F32)


def iota(dims, axis):
    return lax.broadcasted_iota(jnp.int32, dims, axis)


def pick(target, rows=ROWS, first=0):
    span = target.shape[1]
    return (iota((rows, span), 0) + first == target).astype(F32).astype(BF)


def slots(onehots):
    total = sum(onehots)
    span = total.shape[1]
    before = (iota((span, span), 0) < iota((span, span), 1)).astype(F32).astype(BF)
    earlier = nn(total.astype(BF), before)
    return [jnp.sum(o * earlier, axis=0, keepdims=True).astype(jnp.int32) for o in onehots]


def place_body(experts, lengths, languages, enc, dec, sent, enc_at, dec_at):
    enc_count = enc.shape[1]
    dec_count = dec.shape[1]
    rank = iota((EXPERTS, enc_count), 0)
    named = [experts[k : k + 1, :] for k in range(2)]
    found = slots([(rank == e).astype(F32) for e in named])
    targets = [e * CAP + s for e, s in zip(named, found)]
    for k in range(2):
        enc_at[k : k + 1, :] = targets[k]

    sents = lengths.shape[1]
    square = (sents, sents)
    upto = iota(square, 1) <= iota(square, 0)
    same = iota(square, 1) == iota(square, 0)
    length = jnp.broadcast_to(lengths[...], square)
    language = jnp.broadcast_to(languages[...], square)
    ends = jnp.sum(jnp.where(upto, length, 0), axis=1, keepdims=True)
    begins = ends - jnp.sum(jnp.where(same, length, 0), axis=1, keepdims=True)
    spoken = jnp.sum(jnp.where(same, language, 0), axis=1, keepdims=True)
    places = iota((sents, dec_count), 1)
    member = (places >= begins) & (places < ends)
    chosen = jnp.sum(jnp.where(member, spoken, 0), axis=0, keepdims=True)
    dec_onehot = (iota((EXPERTS, dec_count), 0) == chosen).astype(F32)
    (dec_slot,) = slots([dec_onehot])
    dec_target = chosen * CAP + dec_slot
    dec_at[...] = dec_target

    zeros_enc = jnp.zeros((FEATS, enc_count), BF)
    zeros_dec = jnp.zeros((FEATS, dec_count), BF)
    wide_enc = jnp.concatenate([enc[...], zeros_enc], axis=0)
    wide_dec = jnp.concatenate([zeros_dec, dec[...]], axis=0)
    enc_pick = pick(targets[0]) + pick(targets[1])
    rows = nt(enc_pick, wide_enc) + nt(pick(dec_target), wide_dec)
    sent[:, :CAP, :] = rows.astype(BF).reshape(EXPERTS, CAP, 2 * FEATS)
    wide = (EXPERTS, 2 * FEATS)
    counts = jnp.broadcast_to(jnp.sum(dec_onehot, axis=1, keepdims=True), wide)
    on_lanes = jnp.sum(jnp.where(iota(wide, 0) == iota(wide, 1), counts, 0.0), axis=0, keepdims=True)
    for e in range(EXPERTS):
        line = iota((LINES - CAP, 2 * FEATS), 0)
        here = jnp.where(line == 0, on_lanes, jnp.where(line == 1, counts[e : e + 1], 0.0))
        sent[e, CAP:, :] = here.astype(BF)


def spread_body(got, enc, dec, rest, dec_at, most):
    turned = got[:, :CAP, :].reshape(ROWS, 2 * FEATS).astype(F32).T.astype(BF)
    tail = got[:, CAP:, :].astype(F32)
    totals = jnp.sum(tail[:, 0, :], axis=0, keepdims=True)
    most[0] = jnp.max(totals).astype(jnp.int32)
    counts = tail[:, 1, 0:1]
    group = iota((EXPERTS, ROWS), 1) // CAP
    own = jnp.sum(jnp.where(group == iota((EXPERTS, ROWS), 0), counts, 0.0), axis=0, keepdims=True)
    ahead = jnp.sum(jnp.where(group > iota((EXPERTS, ROWS), 0), counts, 0.0), axis=0, keepdims=True)
    slot = iota((1, ROWS), 1) % CAP
    at = jnp.where(slot < own.astype(jnp.int32), ahead.astype(jnp.int32) + slot, -1)
    dec_at[...] = at
    near = nt(turned[FEATS:], pick(at, HELD)).astype(BF)
    far = nt(turned[FEATS:], pick(at, ROWS - HELD, HELD)).astype(BF)
    for t in range(T):
        enc[t] = turned[:FEATS]
        dec[t] = near
        rest[t] = far


def turn_body(w_in, w_out, in_turned, out_turned):
    for d in range(DP):
        cut = [(t * DP + d) * FEATS for t in range(T)]
        block = jnp.concatenate([w_in[c : c + FEATS, :] for c in cut], axis=0)
        in_turned[d] = block.T
    for c in range(16):
        turned = w_out[:, c * 128 : (c + 1) * 128].T
        for half in range(2):
            b = c * 2 + half
            t, d = b // DP, b % DP
            out_turned[d, t * FEATS : (t + 1) * FEATS, :] = turned[half * FEATS : (half + 1) * FEATS]


def expert_body(me, x0, x1, x2, x3, w_in, w_out, p0, p1, p2, p3):
    d = me[0]
    hidden = None
    for k, x in enumerate((x0, x1, x2, x3)):
        source = lax.rem(d - k + DP, DP)
        term = nn(w_in[source], x[...])
        hidden = term if hidden is None else hidden + term
    hidden = jnp.maximum(hidden, 0.0).astype(BF)
    for k, p in enumerate((p0, p1, p2, p3)):
        goal = lax.rem(d + k, DP)
        p[...] = nn(w_out[goal], hidden).astype(BF)


def add_body(a, b, c, d, out):
    total = (a[...].astype(F32) + b[...].astype(F32)) + (c[...].astype(F32) + d[...].astype(F32))
    out[...] = total.astype(BF)


def total(ref):
    acc = ref[0].astype(F32)
    for t in range(1, T):
        acc = acc + ref[t].astype(F32)
    return acc.astype(BF)


def pack_body(enc, dec, rest, dec_at, sent):
    at = dec_at[...]
    back = nn(total(dec), pick(at, HELD)) + nn(total(rest), pick(at, ROWS - HELD, HELD))
    both = jnp.concatenate([total(enc).astype(F32), back], axis=0)
    sent[...] = both.T.astype(BF).reshape(EXPERTS, CAP, 2 * FEATS)


def mix_body(got, enc_at, dec_at, levels, enc, dec, enc_out, dec_out):
    turned = got[...].reshape(ROWS, 2 * FEATS).astype(F32).T.astype(BF)
    level = levels[...].astype(F32)
    whole = level[0:1] + level[1:2]
    mixed = enc[...].astype(F32)
    for k in range(2):
        rows = nn(turned[:FEATS], pick(enc_at[k : k + 1, :]))
        mixed = mixed + (level[k : k + 1] / whole) * rows
    enc_out[...] = mixed.astype(BF)
    rows = nn(turned[FEATS:], pick(dec_at[...]))
    dec_out[...] = (dec[...].astype(F32) + rows).astype(BF)


def shift(value, k):
    return lax.ppermute(value, "dp", [(i, (i + k) % DP) for i in range(DP)])


def over_tensor(block):
    return lax.all_to_all(block, "tensor", split_axis=0, concat_axis=0, tiled=True)


def gather(over_t):
    own = over_t.reshape(T * FEATS, over_t.shape[2])
    return [own] + [shift(own, k) for k in (1, 2, 3)]


def expert(blocks, turned, me):
    rows = blocks[0].shape[1]
    part = shape((T * FEATS, rows))
    work = 4 * rows * UNITS * T * DP * FEATS
    return call(expert_body, [part] * 4, 7, smem=(0,), flops=work, moved=6 << 20)(me, *blocks, *turned)


def scatter(parts):
    rows = parts[0].shape[1]
    sums = [parts[0]] + [shift(parts[k], k) for k in (1, 2, 3)]
    added = call(add_body, shape((T * FEATS, rows)), 4, moved=5 << 19)(*sums)
    return over_tensor(added.reshape(T, FEATS, rows))


def through(block, turned, me):
    return scatter(expert(gather(over_tensor(block)), turned, me))


def shards(
    enc_tokens,
    enc_experts,
    enc_levels,
    enc_w_in,
    enc_w_out,
    dec_tokens,
    dec_lengths,
    dec_language,
    dec_w_in,
    dec_w_out,
):
    me = lax.axis_index("dp").astype(jnp.int32).reshape(1)
    enc = enc_tokens.T
    dec = dec_tokens.T
    packed = shape((EXPERTS, LINES, 2 * FEATS))
    sent, enc_at, dec_at = call(
        place_body,
        [packed, shape((2, enc.shape[1]), jnp.int32), shape((1, dec.shape[1]), jnp.int32)],
        5,
        moved=1 << 18,
    )(enc_experts.T, dec_lengths, dec_language.T, enc, dec)
    got = lax.all_to_all(sent, "expert", split_axis=0, concat_axis=0, tiled=True)

    def turn(w_in, w_out):
        out = [shape((DP, UNITS, T * FEATS)), shape((DP, T * FEATS, UNITS))]
        return call(turn_body, out, 2, moved=4 << 20)(w_in[0], w_out[0])

    enc_turned = turn(enc_w_in, enc_w_out)
    dec_turned = turn(dec_w_in, dec_w_out)
    near = shape((T, FEATS, HELD))
    far = shape((T, FEATS, ROWS - HELD))
    enc_block, dec_block, rest_block, moved_to, most = call(
        spread_body,
        [shape((T, FEATS, ROWS)), near, far, shape((1, ROWS), jnp.int32), shape((1,), jnp.int32)],
        1,
        smem_out=(4,),
        moved=1 << 20,
    )(got)

    enc_t = over_tensor(enc_block)
    dec_block, enc_t = lax.optimization_barrier((dec_block, enc_t))
    dec_t = over_tensor(dec_block)
    enc_x = gather(enc_t)
    dec_x = gather(dec_t)
    enc_sums = scatter(expert(enc_x, enc_turned, me))
    dec_sums = scatter(expert(dec_x, dec_turned, me))
    rest_sums = lax.cond(
        most[0] > HELD,
        lambda b, w: through(b, w, me),
        lambda b, w: jnp.zeros_like(b),
        rest_block,
        dec_turned,
    )

    packed = shape((EXPERTS, CAP, 2 * FEATS))
    back = call(pack_body, packed, 4, moved=1 << 20)(enc_sums, dec_sums, rest_sums, moved_to)
    got = lax.all_to_all(back, "expert", split_axis=0, concat_axis=0, tiled=True)
    enc_out, dec_out = call(
        mix_body, [shape(enc.shape), shape(dec.shape)], 6, moved=1 << 18
    )(got, enc_at, dec_at, enc_levels.T, enc, dec)
    return enc_out.T, dec_out.T


def solution(mesh):
    return jax.shard_map(
        shards,
        mesh=mesh,
        in_specs=(
            P("expert", ("tensor", "dp")),
            P("expert", None),
            P("expert", None),
            P("expert", None, ("tensor", "dp")),
            P("expert", ("tensor", "dp"), None),
            P("expert", ("tensor", "dp")),
            P("expert", None),
            P("expert", None),
            P("expert", None, ("tensor", "dp")),
            P("expert", ("tensor", "dp"), None),
        ),
        out_specs=(P("expert", ("tensor", "dp")), P("expert", ("tensor", "dp"))),
        check_vma=False,
    )
```

```python
import jax
import jax.numpy as jnp
from jax import lax
from jax.experimental import pallas as pl
from jax.experimental.pallas import tpu as pltpu
from jax.sharding import PartitionSpec as P

BF = jnp.bfloat16
F32 = jnp.float32
EXPERTS = 16
CAP = 32
ROWS = EXPERTS * CAP
FEATS = 64
HELD = 256
LINES = CAP + 16
T = 8
DP = 4
UNITS = 256
VMEM = pl.BlockSpec(memory_space=pltpu.VMEM)
SMEM = pl.BlockSpec(memory_space=pltpu.SMEM)


def call(body, out_shape, n_in, *, smem=(), smem_out=(), flops=0, moved=0):
    many = isinstance(out_shape, (tuple, list))
    outs = [SMEM if i in smem_out else VMEM for i in range(len(out_shape))] if many else VMEM
    return pl.pallas_call(
        body,
        out_shape=out_shape,
        in_specs=[SMEM if i in smem else VMEM for i in range(n_in)],
        out_specs=outs,
        compiler_params=pltpu.CompilerParams(vmem_limit_bytes=32 * 1024 * 1024),
        cost_estimate=pl.CostEstimate(flops=flops, bytes_accessed=moved, transcendentals=0),
    )


def shape(dims, dtype=BF):
    return jax.ShapeDtypeStruct(dims, dtype)


def nt(a, b):
    return lax.dot_general(a, b, (((1,), (1,)), ((), ())), preferred_element_type=F32)


def nn(a, b):
    return lax.dot_general(a, b, (((1,), (0,)), ((), ())), preferred_element_type=F32)


def iota(dims, axis):
    return lax.broadcasted_iota(jnp.int32, dims, axis)


def pick(target, rows=ROWS, first=0):
    span = target.shape[1]
    return (iota((rows, span), 0) + first == target).astype(F32).astype(BF)


def slots(onehots):
    total = sum(onehots)
    span = total.shape[1]
    before = (iota((span, span), 0) < iota((span, span), 1)).astype(F32).astype(BF)
    earlier = nn(total.astype(BF), before)
    return [jnp.sum(o * earlier, axis=0, keepdims=True).astype(jnp.int32) for o in onehots]


def place_body(experts, lengths, languages, enc, dec, sent, enc_at, dec_at):
    enc_count = enc.shape[1]
    dec_count = dec.shape[1]
    rank = iota((EXPERTS, enc_count), 0)
    named = [experts[k : k + 1, :] for k in range(2)]
    found = slots([(rank == e).astype(F32) for e in named])
    targets = [e * CAP + s for e, s in zip(named, found)]
    for k in range(2):
        enc_at[k : k + 1, :] = targets[k]

    sents = lengths.shape[1]
    square = (sents, sents)
    upto = iota(square, 1) <= iota(square, 0)
    same = iota(square, 1) == iota(square, 0)
    length = jnp.broadcast_to(lengths[...], square)
    language = jnp.broadcast_to(languages[...], square)
    ends = jnp.sum(jnp.where(upto, length, 0), axis=1, keepdims=True)
    begins = ends - jnp.sum(jnp.where(same, length, 0), axis=1, keepdims=True)
    spoken = jnp.sum(jnp.where(same, language, 0), axis=1, keepdims=True)
    places = iota((sents, dec_count), 1)
    member = (places >= begins) & (places < ends)
    chosen = jnp.sum(jnp.where(member, spoken, 0), axis=0, keepdims=True)
    dec_onehot = (iota((EXPERTS, dec_count), 0) == chosen).astype(F32)
    (dec_slot,) = slots([dec_onehot])
    dec_target = chosen * CAP + dec_slot
    dec_at[...] = dec_target

    zeros_enc = jnp.zeros((FEATS, enc_count), BF)
    zeros_dec = jnp.zeros((FEATS, dec_count), BF)
    wide_enc = jnp.concatenate([enc[...], zeros_enc], axis=0)
    wide_dec = jnp.concatenate([zeros_dec, dec[...]], axis=0)
    enc_pick = pick(targets[0]) + pick(targets[1])
    rows = nt(enc_pick, wide_enc) + nt(pick(dec_target), wide_dec)
    sent[:, :CAP, :] = rows.astype(BF).reshape(EXPERTS, CAP, 2 * FEATS)
    wide = (EXPERTS, 2 * FEATS)
    counts = jnp.broadcast_to(jnp.sum(dec_onehot, axis=1, keepdims=True), wide)
    on_lanes = jnp.sum(jnp.where(iota(wide, 0) == iota(wide, 1), counts, 0.0), axis=0, keepdims=True)
    for e in range(EXPERTS):
        line = iota((LINES - CAP, 2 * FEATS), 0)
        here = jnp.where(line == 0, on_lanes, jnp.where(line == 1, counts[e : e + 1], 0.0))
        sent[e, CAP:, :] = here.astype(BF)


def spread_body(got, enc_a, enc_b, dec, rest, dec_at, most):
    turned = got[:, :CAP, :].reshape(ROWS, 2 * FEATS).astype(F32).T.astype(BF)
    tail = got[:, CAP:, :].astype(F32)
    totals = jnp.sum(tail[:, 0, :], axis=0, keepdims=True)
    most[0] = jnp.max(totals).astype(jnp.int32)
    counts = tail[:, 1, 0:1]
    group = iota((EXPERTS, ROWS), 1) // CAP
    own = jnp.sum(jnp.where(group == iota((EXPERTS, ROWS), 0), counts, 0.0), axis=0, keepdims=True)
    ahead = jnp.sum(jnp.where(group > iota((EXPERTS, ROWS), 0), counts, 0.0), axis=0, keepdims=True)
    slot = iota((1, ROWS), 1) % CAP
    at = jnp.where(slot < own.astype(jnp.int32), ahead.astype(jnp.int32) + slot, -1)
    dec_at[...] = at
    near = nt(turned[FEATS:], pick(at, HELD)).astype(BF)
    far = nt(turned[FEATS:], pick(at, ROWS - HELD, HELD)).astype(BF)
    for t in range(T):
        enc_a[t] = turned[:FEATS, :HELD]
        enc_b[t] = turned[:FEATS, HELD:]
        dec[t] = near
        rest[t] = far


def turn_body(w_in, w_out, in_turned, out_turned):
    for d in range(DP):
        cut = [(t * DP + d) * FEATS for t in range(T)]
        block = jnp.concatenate([w_in[c : c + FEATS, :] for c in cut], axis=0)
        in_turned[d] = block.T
    for c in range(16):
        turned = w_out[:, c * 128 : (c + 1) * 128].T
        for half in range(2):
            b = c * 2 + half
            t, d = b // DP, b % DP
            out_turned[d, t * FEATS : (t + 1) * FEATS, :] = turned[half * FEATS : (half + 1) * FEATS]


def expert_body(me, x0, x1, x2, x3, w_in, w_out, p0, p1, p2, p3):
    d = me[0]
    hidden = None
    for k, x in enumerate((x0, x1, x2, x3)):
        source = lax.rem(d - k + DP, DP)
        term = nn(w_in[source], x[...])
        hidden = term if hidden is None else hidden + term
    hidden = jnp.maximum(hidden, 0.0).astype(BF)
    for k, p in enumerate((p0, p1, p2, p3)):
        goal = lax.rem(d + k, DP)
        p[...] = nn(w_out[goal], hidden).astype(BF)


def add_body(a, b, c, d, out):
    total = (a[...].astype(F32) + b[...].astype(F32)) + (c[...].astype(F32) + d[...].astype(F32))
    out[...] = total.astype(BF)


def total(ref):
    acc = ref[0].astype(F32)
    for t in range(1, T):
        acc = acc + ref[t].astype(F32)
    return acc.astype(BF)


def pack_body(enc_a, enc_b, dec, rest, dec_at, sent):
    at = dec_at[...]
    back = nn(total(dec), pick(at, HELD)) + nn(total(rest), pick(at, ROWS - HELD, HELD))
    enc = jnp.concatenate([total(enc_a), total(enc_b)], axis=1).astype(F32)
    both = jnp.concatenate([enc, back], axis=0)
    sent[...] = both.T.astype(BF).reshape(EXPERTS, CAP, 2 * FEATS)


def mix_body(got, enc_at, dec_at, levels, enc, dec, enc_out, dec_out):
    turned = got[...].reshape(ROWS, 2 * FEATS).astype(F32).T.astype(BF)
    level = levels[...].astype(F32)
    whole = level[0:1] + level[1:2]
    mixed = enc[...].astype(F32)
    for k in range(2):
        rows = nn(turned[:FEATS], pick(enc_at[k : k + 1, :]))
        mixed = mixed + (level[k : k + 1] / whole) * rows
    enc_out[...] = mixed.astype(BF)
    rows = nn(turned[FEATS:], pick(dec_at[...]))
    dec_out[...] = (dec[...].astype(F32) + rows).astype(BF)


def shift(value, k):
    return lax.ppermute(value, "dp", [(i, (i + k) % DP) for i in range(DP)])


def over_tensor(block):
    return lax.all_to_all(block, "tensor", split_axis=0, concat_axis=0, tiled=True)


def gather(over_t):
    own = over_t.reshape(T * FEATS, over_t.shape[2])
    return [own] + [shift(own, k) for k in (1, 2, 3)]


def expert(blocks, turned, me):
    rows = blocks[0].shape[1]
    part = shape((T * FEATS, rows))
    work = 4 * rows * UNITS * T * DP * FEATS
    return call(expert_body, [part] * 4, 7, smem=(0,), flops=work, moved=6 << 20)(me, *blocks, *turned)


def scatter(parts):
    rows = parts[0].shape[1]
    sums = [parts[0]] + [shift(parts[k], k) for k in (1, 2, 3)]
    added = call(add_body, shape((T * FEATS, rows)), 4, moved=5 << 19)(*sums)
    return over_tensor(added.reshape(T, FEATS, rows))


def through(block, turned, me):
    return scatter(expert(gather(over_tensor(block)), turned, me))


def shards(
    enc_tokens,
    enc_experts,
    enc_levels,
    enc_w_in,
    enc_w_out,
    dec_tokens,
    dec_lengths,
    dec_language,
    dec_w_in,
    dec_w_out,
):
    me = lax.axis_index("dp").astype(jnp.int32).reshape(1)
    enc = enc_tokens.T
    dec = dec_tokens.T
    packed = shape((EXPERTS, LINES, 2 * FEATS))
    sent, enc_at, dec_at = call(
        place_body,
        [packed, shape((2, enc.shape[1]), jnp.int32), shape((1, dec.shape[1]), jnp.int32)],
        5,
        moved=1 << 18,
    )(enc_experts.T, dec_lengths, dec_language.T, enc, dec)
    got = lax.all_to_all(sent, "expert", split_axis=0, concat_axis=0, tiled=True)

    def turn(w_in, w_out):
        out = [shape((DP, UNITS, T * FEATS)), shape((DP, T * FEATS, UNITS))]
        return call(turn_body, out, 2, moved=4 << 20)(w_in[0], w_out[0])

    enc_turned = turn(enc_w_in, enc_w_out)
    dec_turned = turn(dec_w_in, dec_w_out)
    near = shape((T, FEATS, HELD))
    far = shape((T, FEATS, ROWS - HELD))
    *blocks, rest_block, moved_to, most = call(
        spread_body,
        [near, far, near, far, shape((1, ROWS), jnp.int32), shape((1,), jnp.int32)],
        1,
        smem_out=(5,),
        moved=1 << 20,
    )(got)

    weights = [enc_turned, enc_turned, dec_turned]
    sums = [through(block, turned, me) for block, turned in zip(blocks, weights)]
    rest_sums = lax.cond(
        most[0] > HELD,
        lambda b, w: through(b, w, me),
        lambda b, w: jnp.zeros_like(b),
        rest_block,
        dec_turned,
    )

    packed = shape((EXPERTS, CAP, 2 * FEATS))
    back = call(pack_body, packed, 5, moved=1 << 20)(*sums, rest_sums, moved_to)
    got = lax.all_to_all(back, "expert", split_axis=0, concat_axis=0, tiled=True)
    enc_out, dec_out = call(
        mix_body, [shape(enc.shape), shape(dec.shape)], 6, moved=1 << 18
    )(got, enc_at, dec_at, enc_levels.T, enc, dec)
    return enc_out.T, dec_out.T


def solution(mesh):
    return jax.shard_map(
        shards,
        mesh=mesh,
        in_specs=(
            P("expert", ("tensor", "dp")),
            P("expert", None),
            P("expert", None),
            P("expert", None, ("tensor", "dp")),
            P("expert", ("tensor", "dp"), None),
            P("expert", ("tensor", "dp")),
            P("expert", None),
            P("expert", None),
            P("expert", None, ("tensor", "dp")),
            P("expert", ("tensor", "dp"), None),
        ),
        out_specs=(P("expert", ("tensor", "dp")), P("expert", ("tensor", "dp"))),
        check_vma=False,
    )
```

```python
import jax
import jax.numpy as jnp
from jax import lax
from jax.experimental import pallas as pl
from jax.experimental.pallas import tpu as pltpu
from jax.sharding import PartitionSpec as P

BF = jnp.bfloat16
F32 = jnp.float32
EXPERTS = 16
CAP = 32
ROWS = EXPERTS * CAP
FEATS = 64
HELD = 256
LINES = CAP + 16
T = 8
DP = 4
UNITS = 256
VMEM = pl.BlockSpec(memory_space=pltpu.VMEM)
SMEM = pl.BlockSpec(memory_space=pltpu.SMEM)


def call(body, out_shape, n_in, *, smem=(), smem_out=(), flops=0, moved=0):
    many = isinstance(out_shape, (tuple, list))
    outs = [SMEM if i in smem_out else VMEM for i in range(len(out_shape))] if many else VMEM
    return pl.pallas_call(
        body,
        out_shape=out_shape,
        in_specs=[SMEM if i in smem else VMEM for i in range(n_in)],
        out_specs=outs,
        compiler_params=pltpu.CompilerParams(vmem_limit_bytes=32 * 1024 * 1024),
        cost_estimate=pl.CostEstimate(flops=flops, bytes_accessed=moved, transcendentals=0),
    )


def shape(dims, dtype=BF):
    return jax.ShapeDtypeStruct(dims, dtype)


def nt(a, b):
    return lax.dot_general(a, b, (((1,), (1,)), ((), ())), preferred_element_type=F32)


def nn(a, b):
    return lax.dot_general(a, b, (((1,), (0,)), ((), ())), preferred_element_type=F32)


def iota(dims, axis):
    return lax.broadcasted_iota(jnp.int32, dims, axis)


def pick(target, rows=ROWS, first=0):
    span = target.shape[1]
    return (iota((rows, span), 0) + first == target).astype(F32).astype(BF)


def slots(onehots):
    total = sum(onehots)
    span = total.shape[1]
    before = (iota((span, span), 0) < iota((span, span), 1)).astype(F32).astype(BF)
    earlier = nn(total.astype(BF), before)
    return [jnp.sum(o * earlier, axis=0, keepdims=True).astype(jnp.int32) for o in onehots]


def place_body(experts, lengths, languages, enc, dec, sent, enc_at, dec_at):
    enc_count = enc.shape[1]
    dec_count = dec.shape[1]
    rank = iota((EXPERTS, enc_count), 0)
    named = [experts[k : k + 1, :] for k in range(2)]
    found = slots([(rank == e).astype(F32) for e in named])
    targets = [e * CAP + s for e, s in zip(named, found)]
    for k in range(2):
        enc_at[k : k + 1, :] = targets[k]

    sents = lengths.shape[1]
    square = (sents, sents)
    upto = iota(square, 1) <= iota(square, 0)
    same = iota(square, 1) == iota(square, 0)
    length = jnp.broadcast_to(lengths[...], square)
    language = jnp.broadcast_to(languages[...], square)
    ends = jnp.sum(jnp.where(upto, length, 0), axis=1, keepdims=True)
    begins = ends - jnp.sum(jnp.where(same, length, 0), axis=1, keepdims=True)
    spoken = jnp.sum(jnp.where(same, language, 0), axis=1, keepdims=True)
    places = iota((sents, dec_count), 1)
    member = (places >= begins) & (places < ends)
    chosen = jnp.sum(jnp.where(member, spoken, 0), axis=0, keepdims=True)
    dec_onehot = (iota((EXPERTS, dec_count), 0) == chosen).astype(F32)
    (dec_slot,) = slots([dec_onehot])
    dec_target = chosen * CAP + dec_slot
    dec_at[...] = dec_target

    zeros_enc = jnp.zeros((FEATS, enc_count), BF)
    zeros_dec = jnp.zeros((FEATS, dec_count), BF)
    wide_enc = jnp.concatenate([enc[...], zeros_enc], axis=0)
    wide_dec = jnp.concatenate([zeros_dec, dec[...]], axis=0)
    enc_pick = pick(targets[0]) + pick(targets[1])
    rows = nt(enc_pick, wide_enc) + nt(pick(dec_target), wide_dec)
    sent[:, :CAP, :] = rows.astype(BF).reshape(EXPERTS, CAP, 2 * FEATS)
    wide = (EXPERTS, 2 * FEATS)
    counts = jnp.broadcast_to(jnp.sum(dec_onehot, axis=1, keepdims=True), wide)
    on_lanes = jnp.sum(jnp.where(iota(wide, 0) == iota(wide, 1), counts, 0.0), axis=0, keepdims=True)
    for e in range(EXPERTS):
        line = iota((LINES - CAP, 2 * FEATS), 0)
        here = jnp.where(line == 0, on_lanes, jnp.where(line == 1, counts[e : e + 1], 0.0))
        sent[e, CAP:, :] = here.astype(BF)


def spread_body(got, enc, dec, rest, dec_at, most):
    turned = got[:, :CAP, :].reshape(ROWS, 2 * FEATS).astype(F32).T.astype(BF)
    tail = got[:, CAP:, :].astype(F32)
    totals = jnp.sum(tail[:, 0, :], axis=0, keepdims=True)
    most[0] = jnp.max(totals).astype(jnp.int32)
    counts = tail[:, 1, 0:1]
    group = iota((EXPERTS, ROWS), 1) // CAP
    own = jnp.sum(jnp.where(group == iota((EXPERTS, ROWS), 0), counts, 0.0), axis=0, keepdims=True)
    ahead = jnp.sum(jnp.where(group > iota((EXPERTS, ROWS), 0), counts, 0.0), axis=0, keepdims=True)
    slot = iota((1, ROWS), 1) % CAP
    at = jnp.where(slot < own.astype(jnp.int32), ahead.astype(jnp.int32) + slot, -1)
    dec_at[...] = at
    near = nt(turned[FEATS:], pick(at, HELD)).astype(BF)
    far = nt(turned[FEATS:], pick(at, ROWS - HELD, HELD)).astype(BF)
    dec[...] = near
    for t in range(T):
        enc[t] = turned[:FEATS]
        rest[t] = far


def turn_body(w_in, w_out, in_turned, out_turned):
    for d in range(DP):
        cut = [(t * DP + d) * FEATS for t in range(T)]
        block = jnp.concatenate([w_in[c : c + FEATS, :] for c in cut], axis=0)
        in_turned[d] = block.T
    for c in range(16):
        turned = w_out[:, c * 128 : (c + 1) * 128].T
        for half in range(2):
            b = c * 2 + half
            t, d = b // DP, b % DP
            out_turned[d, t * FEATS : (t + 1) * FEATS, :] = turned[half * FEATS : (half + 1) * FEATS]


def expert_body(me, x0, x1, x2, x3, w_in, w_out, p0, p1, p2, p3):
    d = me[0]
    hidden = None
    for k, x in enumerate((x0, x1, x2, x3)):
        source = lax.rem(d - k + DP, DP)
        term = nn(w_in[source], x[...])
        hidden = term if hidden is None else hidden + term
    hidden = jnp.maximum(hidden, 0.0).astype(BF)
    for k, p in enumerate((p0, p1, p2, p3)):
        goal = lax.rem(d + k, DP)
        p[...] = nn(w_out[goal], hidden).astype(BF)


def add_body(a, b, c, d, out):
    total = (a[...].astype(F32) + b[...].astype(F32)) + (c[...].astype(F32) + d[...].astype(F32))
    out[...] = total.astype(BF)


def total(ref):
    acc = ref[0].astype(F32)
    for t in range(1, T):
        acc = acc + ref[t].astype(F32)
    return acc.astype(BF)


def pack_body(enc, dec_a, dec_b, dec_c, dec_d, rest, dec_at, sent):
    at = dec_at[...]
    dec = sum(ref[...].astype(F32) for ref in (dec_a, dec_b, dec_c, dec_d)).astype(BF)
    back = nn(dec, pick(at, HELD)) + nn(total(rest), pick(at, ROWS - HELD, HELD))
    both = jnp.concatenate([total(enc).astype(F32), back], axis=0)
    sent[...] = both.T.astype(BF).reshape(EXPERTS, CAP, 2 * FEATS)


def mix_body(got, enc_at, dec_at, levels, enc, dec, enc_out, dec_out):
    turned = got[...].reshape(ROWS, 2 * FEATS).astype(F32).T.astype(BF)
    level = levels[...].astype(F32)
    whole = level[0:1] + level[1:2]
    mixed = enc[...].astype(F32)
    for k in range(2):
        rows = nn(turned[:FEATS], pick(enc_at[k : k + 1, :]))
        mixed = mixed + (level[k : k + 1] / whole) * rows
    enc_out[...] = mixed.astype(BF)
    rows = nn(turned[FEATS:], pick(dec_at[...]))
    dec_out[...] = (dec[...].astype(F32) + rows).astype(BF)


def shift(value, k):
    return lax.ppermute(value, "dp", [(i, (i + k) % DP) for i in range(DP)])


def over_tensor(block):
    return lax.all_to_all(block, "tensor", split_axis=0, concat_axis=0, tiled=True)


def gather(over_t):
    own = over_t.reshape(T * FEATS, over_t.shape[2])
    return [own] + [shift(own, k) for k in (1, 2, 3)]


def expert(blocks, turned, me):
    rows = blocks[0].shape[1]
    part = shape((T * FEATS, rows))
    work = 4 * rows * UNITS * T * DP * FEATS
    return call(expert_body, [part] * 4, 7, smem=(0,), flops=work, moved=6 << 20)(me, *blocks, *turned)


def arrive(parts):
    return [parts[0]] + [shift(parts[k], k) for k in (1, 2, 3)]


def settle(parts):
    rows = parts[0].shape[1]
    added = call(add_body, shape((T * FEATS, rows)), 4, moved=5 << 19)(*parts)
    return over_tensor(added.reshape(T, FEATS, rows))


def through(block, turned, me):
    return settle(arrive(expert(gather(over_tensor(block)), turned, me)))


def tie(values, others):
    done = lax.optimization_barrier((list(values), list(others)))
    return done[0], done[1]


def copies_body(a, b, c, d, out):
    for t in range(T):
        for k, ref in enumerate((a, b, c, d)):
            out[t, k] = ref[...]


def crossed_body(me, x, w_in, w_out, part):
    d = me[0]
    rows = x.shape[3]
    hidden = None
    for k in range(DP):
        block = x[:, k].reshape(T * FEATS, rows)
        term = nn(w_in[lax.rem(d - k + DP, DP)], block)
        hidden = term if hidden is None else hidden + term
    hidden = jnp.maximum(hidden, 0.0).astype(BF)
    for k in range(DP):
        block = nn(w_out[lax.rem(d + k, DP)], hidden).astype(BF)
        part[:, k] = block.reshape(T, FEATS, rows)


def crossed_sum_body(got, a, b, c, d):
    for k, ref in enumerate((a, b, c, d)):
        acc = got[0, k].astype(F32)
        for t in range(1, T):
            acc = acc + got[t, k].astype(F32)
        ref[...] = acc.astype(BF)


def expert_crossed(x, turned, me):
    work = 4 * x.shape[3] * UNITS * T * DP * FEATS
    return call(crossed_body, shape(x.shape), 4, smem=(0,), flops=work, moved=4 << 20)(me, x, *turned)


def shards(
    enc_tokens,
    enc_experts,
    enc_levels,
    enc_w_in,
    enc_w_out,
    dec_tokens,
    dec_lengths,
    dec_language,
    dec_w_in,
    dec_w_out,
):
    me = lax.axis_index("dp").astype(jnp.int32).reshape(1)
    enc = enc_tokens.T
    dec = dec_tokens.T
    packed = shape((EXPERTS, LINES, 2 * FEATS))
    sent, enc_at, dec_at = call(
        place_body,
        [packed, shape((2, enc.shape[1]), jnp.int32), shape((1, dec.shape[1]), jnp.int32)],
        5,
        moved=1 << 18,
    )(enc_experts.T, dec_lengths, dec_language.T, enc, dec)
    got = lax.all_to_all(sent, "expert", split_axis=0, concat_axis=0, tiled=True)

    def turn(w_in, w_out):
        out = [shape((DP, UNITS, T * FEATS)), shape((DP, T * FEATS, UNITS))]
        return call(turn_body, out, 2, moved=4 << 20)(w_in[0], w_out[0])

    enc_turned = turn(enc_w_in, enc_w_out)
    dec_turned = turn(dec_w_in, dec_w_out)
    far = shape((T, FEATS, ROWS - HELD))
    enc_block, dec_block, rest_block, moved_to, most = call(
        spread_body,
        [shape((T, FEATS, ROWS)), shape((FEATS, HELD)), far, shape((1, ROWS), jnp.int32), shape((1,), jnp.int32)],
        1,
        smem_out=(4,),
        moved=1 << 20,
    )(got)

    near_x = [dec_block] + [shift(dec_block, k) for k in (1, 2, 3)]
    dec_x = call(copies_body, shape((T, DP, FEATS, HELD)), 4, moved=1 << 20)(*near_x)
    enc_t = over_tensor(enc_block)
    (dec_x,), (enc_t,) = tie([dec_x], [enc_t])
    enc_x = gather(enc_t)
    dec_x = over_tensor(dec_x)
    (dec_x,), enc_x = tie([dec_x], enc_x)
    dec_parts = expert_crossed(dec_x, dec_turned, me)
    enc_got = arrive(expert(enc_x, enc_turned, me))
    dec_parts = over_tensor(dec_parts)
    (dec_parts,), (enc_got[0],) = tie([dec_parts], [enc_got[0]])
    dec_parts = call(crossed_sum_body, [shape((FEATS, HELD))] * 4, 1, moved=1 << 20)(dec_parts)
    dec_sums = arrive(dec_parts)
    enc_sums = settle(enc_got)
    rest_sums = lax.cond(
        most[0] > HELD,
        lambda b, w: through(b, w, me),
        lambda b, w: jnp.zeros_like(b),
        rest_block,
        dec_turned,
    )

    packed = shape((EXPERTS, CAP, 2 * FEATS))
    back = call(pack_body, packed, 7, moved=1 << 20)(enc_sums, *dec_sums, rest_sums, moved_to)
    got = lax.all_to_all(back, "expert", split_axis=0, concat_axis=0, tiled=True)
    enc_out, dec_out = call(
        mix_body, [shape(enc.shape), shape(dec.shape)], 6, moved=1 << 18
    )(got, enc_at, dec_at, enc_levels.T, enc, dec)
    return enc_out.T, dec_out.T


def solution(mesh):
    return jax.shard_map(
        shards,
        mesh=mesh,
        in_specs=(
            P("expert", ("tensor", "dp")),
            P("expert", None),
            P("expert", None),
            P("expert", None, ("tensor", "dp")),
            P("expert", ("tensor", "dp"), None),
            P("expert", ("tensor", "dp")),
            P("expert", None),
            P("expert", None),
            P("expert", None, ("tensor", "dp")),
            P("expert", ("tensor", "dp"), None),
        ),
        out_specs=(P("expert", ("tensor", "dp")), P("expert", ("tensor", "dp"))),
        check_vma=False,
    )
```

```python
import jax
import jax.numpy as jnp
from jax import lax
from jax.experimental import pallas as pl
from jax.experimental.pallas import tpu as pltpu
from jax.sharding import PartitionSpec as P

BF = jnp.bfloat16
F32 = jnp.float32
EXPERTS = 16
CAP = 32
ROWS = EXPERTS * CAP
FEATS = 64
HELD = 256
LINES = CAP + 16
T = 8
DP = 4
UNITS = 256
VMEM = pl.BlockSpec(memory_space=pltpu.VMEM)
SMEM = pl.BlockSpec(memory_space=pltpu.SMEM)
ANY = pl.BlockSpec(memory_space=pl.ANY)


def call(body, out_shape, n_in, *, smem=(), smem_out=(), limit=32, flops=0, moved=0, after=0, far=(), far_out=False, scratch=()):
    def timed(*refs):
        body(*refs[:n_in], *refs[n_in + after :])

    many = isinstance(out_shape, (tuple, list))
    whole = pl.BlockSpec() if limit > 32 else VMEM
    place = ANY if far_out else whole
    outs = [SMEM if i in smem_out else place for i in range(len(out_shape))] if many else place
    return pl.pallas_call(
        timed,
        out_shape=out_shape,
        in_specs=[SMEM if i in smem else ANY if i in far else whole for i in range(n_in)] + [ANY] * after,
        scratch_shapes=list(scratch),
        out_specs=outs,
        compiler_params=pltpu.CompilerParams(vmem_limit_bytes=limit * 1024 * 1024),
        cost_estimate=pl.CostEstimate(flops=flops, bytes_accessed=moved, transcendentals=0),
    )


def shape(dims, dtype=BF):
    return jax.ShapeDtypeStruct(dims, dtype)


def nt(a, b):
    return lax.dot_general(a, b, (((1,), (1,)), ((), ())), preferred_element_type=F32)


def nn(a, b):
    return lax.dot_general(a, b, (((1,), (0,)), ((), ())), preferred_element_type=F32)


def iota(dims, axis):
    return lax.broadcasted_iota(jnp.int32, dims, axis)


def pick(target, rows=ROWS, first=0):
    span = target.shape[1]
    return (iota((rows, span), 0) + first == target).astype(F32).astype(BF)


def slots(onehots):
    total = sum(onehots)
    span = total.shape[1]
    before = (iota((span, span), 0) < iota((span, span), 1)).astype(F32).astype(BF)
    earlier = nn(total.astype(BF), before)
    return [jnp.sum(o * earlier, axis=0, keepdims=True).astype(jnp.int32) for o in onehots]


def place_body(experts, lengths, languages, enc, dec, sent, enc_at, dec_at):
    enc_count = enc.shape[1]
    dec_count = dec.shape[1]
    rank = iota((EXPERTS, enc_count), 0)
    named = [experts[k : k + 1, :] for k in range(2)]
    found = slots([(rank == e).astype(F32) for e in named])
    targets = [e * CAP + s for e, s in zip(named, found)]
    for k in range(2):
        enc_at[k : k + 1, :] = targets[k]

    sents = lengths.shape[1]
    square = (sents, sents)
    upto = iota(square, 1) <= iota(square, 0)
    same = iota(square, 1) == iota(square, 0)
    length = jnp.broadcast_to(lengths[...], square)
    language = jnp.broadcast_to(languages[...], square)
    ends = jnp.sum(jnp.where(upto, length, 0), axis=1, keepdims=True)
    begins = ends - jnp.sum(jnp.where(same, length, 0), axis=1, keepdims=True)
    spoken = jnp.sum(jnp.where(same, language, 0), axis=1, keepdims=True)
    places = iota((sents, dec_count), 1)
    member = (places >= begins) & (places < ends)
    chosen = jnp.sum(jnp.where(member, spoken, 0), axis=0, keepdims=True)
    dec_onehot = (iota((EXPERTS, dec_count), 0) == chosen).astype(F32)
    (dec_slot,) = slots([dec_onehot])
    dec_target = chosen * CAP + dec_slot
    dec_at[...] = dec_target

    zeros_enc = jnp.zeros((FEATS, enc_count), BF)
    zeros_dec = jnp.zeros((FEATS, dec_count), BF)
    wide_enc = jnp.concatenate([enc[...], zeros_enc], axis=0)
    wide_dec = jnp.concatenate([zeros_dec, dec[...]], axis=0)
    enc_pick = pick(targets[0]) + pick(targets[1])
    rows = nt(enc_pick, wide_enc) + nt(pick(dec_target), wide_dec)
    sent[:, :CAP, :] = rows.astype(BF).reshape(EXPERTS, CAP, 2 * FEATS)
    wide = (EXPERTS, 2 * FEATS)
    counts = jnp.broadcast_to(jnp.sum(dec_onehot, axis=1, keepdims=True), wide)
    on_lanes = jnp.sum(jnp.where(iota(wide, 0) == iota(wide, 1), counts, 0.0), axis=0, keepdims=True)
    for e in range(EXPERTS):
        line = iota((LINES - CAP, 2 * FEATS), 0)
        here = jnp.where(line == 0, on_lanes, jnp.where(line == 1, counts[e : e + 1], 0.0))
        sent[e, CAP:, :] = here.astype(BF)


def spread_body(got, enc, dec, rest, dec_at, most):
    turned = got[:, :CAP, :].reshape(ROWS, 2 * FEATS).astype(F32).T.astype(BF)
    tail = got[:, CAP:, :].astype(F32)
    totals = jnp.sum(tail[:, 0, :], axis=0, keepdims=True)
    most[0] = jnp.max(totals).astype(jnp.int32)
    counts = tail[:, 1, 0:1]
    group = iota((EXPERTS, ROWS), 1) // CAP
    own = jnp.sum(jnp.where(group == iota((EXPERTS, ROWS), 0), counts, 0.0), axis=0, keepdims=True)
    ahead = jnp.sum(jnp.where(group > iota((EXPERTS, ROWS), 0), counts, 0.0), axis=0, keepdims=True)
    slot = iota((1, ROWS), 1) % CAP
    at = jnp.where(slot < own.astype(jnp.int32), ahead.astype(jnp.int32) + slot, -1)
    dec_at[...] = at
    near = nt(turned[FEATS:], pick(at, HELD)).astype(BF)
    far = nt(turned[FEATS:], pick(at, ROWS - HELD, HELD)).astype(BF)
    dec[...] = near
    for t in range(T):
        enc[t] = turned[:FEATS]
        rest[t] = far


def turn_body(w_in, w_out, in_turned, out_turned, ready):
    ready[...] = jnp.zeros_like(ready)
    for d in range(DP):
        cut = [(t * DP + d) * FEATS for t in range(T)]
        block = jnp.concatenate([w_in[c : c + FEATS, :] for c in cut], axis=0)
        in_turned[d] = block.T
    for c in range(16):
        turned = w_out[:, c * 128 : (c + 1) * 128].T
        for half in range(2):
            b = c * 2 + half
            t, d = b // DP, b % DP
            out_turned[d, t * FEATS : (t + 1) * FEATS, :] = turned[half * FEATS : (half + 1) * FEATS]


def turn_near_body(me, w_in, w_out, in_turned, out_turned, ready):
    ready[...] = jnp.zeros_like(ready)
    span = DP * FEATS
    for t in range(T):
        for k in range(DP):
            at = pl.multiple_of((t * DP + lax.rem(me[0] - k + DP, DP)) * FEATS, FEATS)
            to = t * span + k * FEATS
            out_turned[to : to + FEATS, :] = w_in[pl.ds(at, FEATS), :]
    ordered = out_turned[...]
    in_turned[...] = ordered.T
    for t in range(T):
        block = w_out[:, t * span : (t + 1) * span].T
        for k in range(DP):
            to = pl.multiple_of(t * span + lax.rem(k - me[0] + DP, DP) * FEATS, FEATS)
            out_turned[pl.ds(to, FEATS), :] = block[k * FEATS : (k + 1) * FEATS]


def expert_body(me, x0, x1, x2, x3, w_in, w_out, p0, p1, p2, p3, xs, ins, outs, ps, sems):
    d = me[0]
    near = []
    for k, x in enumerate((x0, x1, x2, x3)):
        source = lax.rem(d - k + DP, DP)
        near.append(pltpu.make_async_copy(w_in.at[source], ins.at[k], sems.at[k]))
        near.append(pltpu.make_async_copy(x, xs.at[k], sems.at[DP + k]))
    far = {}
    for k in (2, 1, 3, 0):
        goal = lax.rem(d + k, DP)
        far[k] = pltpu.make_async_copy(w_out.at[goal], outs.at[k], sems.at[2 * DP + k])
    for copy in near + list(far.values()):
        copy.start()
    hidden = None
    for k in range(DP):
        near[2 * k].wait()
        near[2 * k + 1].wait()
        term = nn(ins[k], xs[k])
        hidden = term if hidden is None else hidden + term
    hidden = jnp.maximum(hidden, 0.0).astype(BF)
    gone = []
    for k in (2, 1, 3, 0):
        far[k].wait()
        ps[k] = nn(outs[k], hidden).astype(BF)
        gone.append(pltpu.make_async_copy(ps.at[k], (p0, p1, p2, p3)[k], sems.at[3 * DP + k]))
        gone[-1].start()
    for copy in gone:
        copy.wait()


def add_body(a, b, c, d, out):
    total = (a[...].astype(F32) + b[...].astype(F32)) + (c[...].astype(F32) + d[...].astype(F32))
    out[...] = total.astype(BF)


def total(ref):
    acc = ref[0].astype(F32)
    for t in range(1, T):
        acc = acc + ref[t].astype(F32)
    return acc.astype(BF)


def pack_body(enc, dec_a, dec_b, dec_c, dec_d, rest, dec_at, sent):
    at = dec_at[...]
    dec = sum(ref[...].astype(F32) for ref in (dec_a, dec_b, dec_c, dec_d)).astype(BF)
    back = nn(dec, pick(at, HELD)) + nn(total(rest), pick(at, ROWS - HELD, HELD))
    both = jnp.concatenate([total(enc).astype(F32), back], axis=0)
    sent[...] = both.T.astype(BF).reshape(EXPERTS, CAP, 2 * FEATS)


def mix_body(got, enc_at, dec_at, levels, enc, dec, enc_out, dec_out):
    turned = got[...].reshape(ROWS, 2 * FEATS).astype(F32).T.astype(BF)
    level = levels[...].astype(F32)
    whole = level[0:1] + level[1:2]
    mixed = enc[...].astype(F32)
    for k in range(2):
        rows = nn(turned[:FEATS], pick(enc_at[k : k + 1, :]))
        mixed = mixed + (level[k : k + 1] / whole) * rows
    enc_out[...] = mixed.astype(BF)
    rows = nn(turned[FEATS:], pick(dec_at[...]))
    dec_out[...] = (dec[...].astype(F32) + rows).astype(BF)


def shift(value, k):
    return lax.ppermute(value, "dp", [(i, (i + k) % DP) for i in range(DP)])


def over_tensor(block):
    return lax.all_to_all(block, "tensor", split_axis=0, concat_axis=0, tiled=True)


def gather(over_t):
    own = over_t.reshape(T * FEATS, over_t.shape[2])
    return [own] + [shift(own, k) for k in (1, 2, 3)]


def expert(blocks, turned, me):
    rows = blocks[0].shape[1]
    part = shape((T * FEATS, rows))
    work = 4 * rows * UNITS * T * DP * FEATS
    held = pltpu.VMEM((DP, T * FEATS, rows), BF)
    return call(
        expert_body,
        [part] * 4,
        7,
        smem=(0,),
        far=range(1, 7),
        far_out=True,
        scratch=[held, *(pltpu.VMEM(w.shape, BF) for w in turned), held, pltpu.SemaphoreType.DMA((4 * DP,))],
        limit=60,
        flops=work,
        moved=6 << 20,
    )(me, *blocks, *turned)


def arrive(parts):
    return [parts[0]] + [shift(parts[k], k) for k in (1, 2, 3)]


def settle(parts, later=()):
    rows = parts[0].shape[1]
    added = call(
        add_body, shape((T * FEATS, rows)), 4, moved=5 << 19, after=len(later)
    )(*parts, *later)
    return over_tensor(added.reshape(T, FEATS, rows))


def through(block, turned, me):
    return settle(arrive(expert(gather(over_tensor(block)), turned, me)))


def tie(values, others):
    done = lax.optimization_barrier((list(values), list(others)))
    return done[0], done[1]


def copies_body(a, b, c, d, out):
    for t in range(T):
        for k, ref in enumerate((a, b, c, d)):
            out[t, k] = ref[...]


def crossed_body(x, w_in, w_out, part, xs, ins, outs, ps, sems):
    span = T * FEATS
    first = pltpu.make_async_copy(w_in, ins, sems.at[0])
    near = []
    far = []
    for k in range(DP):
        cut = pl.ds(k * span, span)
        near.append(pltpu.make_async_copy(x.at[cut], xs.at[cut], sems.at[1 + k]))
        far.append(pltpu.make_async_copy(w_out.at[cut], outs.at[cut], sems.at[1 + DP + k]))
    for copy in [first] + near + far:
        copy.start()
    first.wait()
    hidden = None
    for k in range(DP):
        near[k].wait()
        term = nn(ins[:, k * span : (k + 1) * span], xs[k * span : (k + 1) * span, :])
        hidden = term if hidden is None else hidden + term
    hidden = jnp.maximum(hidden, 0.0).astype(BF)
    gone = []
    for k in range(DP):
        far[k].wait()
        cut = pl.ds(k * span, span)
        ps[k * span : (k + 1) * span, :] = nn(outs[k * span : (k + 1) * span, :], hidden).astype(BF)
        gone.append(pltpu.make_async_copy(ps.at[cut], part.at[cut], sems.at[1 + 2 * DP + k]))
        gone[-1].start()
    for copy in gone:
        copy.wait()


def crossed_sum_body(got, a, b, c, d):
    for k, ref in enumerate((a, b, c, d)):
        acc = got[0, k].astype(F32)
        for t in range(1, T):
            acc = acc + got[t, k].astype(F32)
        ref[...] = acc.astype(BF)


def expert_crossed(x, turned, later):
    rows = x.shape[3]
    flat = x.reshape(T * DP * FEATS, rows)
    work = 4 * rows * UNITS * T * DP * FEATS
    held = pltpu.VMEM(flat.shape, BF)
    part = call(
        crossed_body,
        shape(flat.shape),
        3,
        far=range(3),
        far_out=True,
        scratch=[held, *(pltpu.VMEM(w.shape, BF) for w in turned), held, pltpu.SemaphoreType.DMA((1 + 3 * DP,))],
        limit=60,
        flops=work,
        moved=4 << 20,
        after=len(later),
    )(flat, *turned, *later)
    return part.reshape(x.shape)


def shards(
    enc_tokens,
    enc_experts,
    enc_levels,
    enc_w_in,
    enc_w_out,
    dec_tokens,
    dec_lengths,
    dec_language,
    dec_w_in,
    dec_w_out,
):
    me = lax.axis_index("dp").astype(jnp.int32).reshape(1)
    enc = enc_tokens.T
    dec = dec_tokens.T
    packed = shape((EXPERTS, LINES, 2 * FEATS))
    sent, enc_at, dec_at = call(
        place_body,
        [packed, shape((2, enc.shape[1]), jnp.int32), shape((1, dec.shape[1]), jnp.int32)],
        5,
        limit=60,
        moved=1 << 18,
    )(enc_experts.T, dec_lengths, dec_language.T, enc, dec)
    got = lax.all_to_all(sent, "expert", split_axis=0, concat_axis=0, tiled=True)

    def turn(w_in, w_out):
        out = [shape((DP, UNITS, T * FEATS)), shape((DP, T * FEATS, UNITS)), shape((16, 128))]
        return call(turn_body, out, 2, limit=60, moved=4 << 20)(w_in[0], w_out[0])

    *enc_turned, enc_ready = turn(enc_w_in, enc_w_out)
    out = [shape((UNITS, T * DP * FEATS)), shape((T * DP * FEATS, UNITS)), shape((16, 128))]
    *near_turned, dec_ready = call(turn_near_body, out, 3, smem=(0,), limit=60, moved=4 << 20)(me, dec_w_in[0], dec_w_out[0])
    far = shape((T, FEATS, ROWS - HELD))
    enc_block, dec_block, rest_block, moved_to, most = call(
        spread_body,
        [shape((T, FEATS, ROWS)), shape((FEATS, HELD)), far, shape((1, ROWS), jnp.int32), shape((1,), jnp.int32)],
        1,
        smem_out=(4,),
        moved=1 << 20,
        after=2,
    )(got, enc_ready, dec_ready)

    near_x = [dec_block] + [shift(dec_block, k) for k in (1, 2, 3)]
    dec_x = call(copies_body, shape((T, DP, FEATS, HELD)), 4, moved=1 << 20)(*near_x)
    enc_t = over_tensor(enc_block)
    (dec_x,), (enc_t,) = tie([dec_x], [enc_t])
    enc_x = gather(enc_t)
    dec_x = over_tensor(dec_x)
    dec_parts = expert_crossed(dec_x, near_turned, enc_x[1:])
    enc_got = arrive(expert(enc_x, enc_turned, me))
    dec_parts = over_tensor(dec_parts)
    dec_halves = call(crossed_sum_body, [shape((FEATS, HELD))] * 4, 1, moved=1 << 20)(dec_parts)
    dec_sums = arrive(dec_halves)
    enc_sums = settle(enc_got, [dec_parts])
    rest_sums = lax.cond(
        most[0] > HELD,
        lambda b, w: through(b, turn(*w)[:2], me),
        lambda b, w: jnp.zeros_like(b),
        rest_block,
        (dec_w_in, dec_w_out),
    )

    packed = shape((EXPERTS, CAP, 2 * FEATS))
    back = call(pack_body, packed, 7, moved=1 << 20)(enc_sums, *dec_sums, rest_sums, moved_to)
    got = lax.all_to_all(back, "expert", split_axis=0, concat_axis=0, tiled=True)
    enc_out, dec_out = call(
        mix_body, [shape(enc.shape), shape(dec.shape)], 6, moved=1 << 18
    )(got, enc_at, dec_at, enc_levels.T, enc, dec)
    return enc_out.T, dec_out.T


def solution(mesh):
    return jax.shard_map(
        shards,
        mesh=mesh,
        in_specs=(
            P("expert", ("tensor", "dp")),
            P("expert", None),
            P("expert", None),
            P("expert", None, ("tensor", "dp")),
            P("expert", ("tensor", "dp"), None),
            P("expert", ("tensor", "dp")),
            P("expert", None),
            P("expert", None),
            P("expert", None, ("tensor", "dp")),
            P("expert", ("tensor", "dp"), None),
        ),
        out_specs=(P("expert", ("tensor", "dp")), P("expert", ("tensor", "dp"))),
        check_vma=False,
    )
```

```python
import jax
import jax.numpy as jnp
from jax import lax
from jax.experimental import pallas as pl
from jax.experimental.pallas import tpu as pltpu
from jax.sharding import PartitionSpec as P

BF = jnp.bfloat16
F32 = jnp.float32
EXPERTS = 16
CAP = 32
ROWS = EXPERTS * CAP
FEATS = 64
HELD = 256
LINES = CAP + 16
T = 8
DP = 4
UNITS = 256
VMEM = pl.BlockSpec(memory_space=pltpu.VMEM)
SMEM = pl.BlockSpec(memory_space=pltpu.SMEM)
ANY = pl.BlockSpec(memory_space=pl.ANY)


def call(body, out_shape, n_in, *, smem=(), smem_out=(), limit=32, flops=0, moved=0, after=0, far=(), far_out=False, scratch=()):
    def timed(*refs):
        body(*refs[:n_in], *refs[n_in + after :])

    many = isinstance(out_shape, (tuple, list))
    whole = pl.BlockSpec() if limit > 32 else VMEM
    place = ANY if far_out else whole
    outs = [SMEM if i in smem_out else place for i in range(len(out_shape))] if many else place
    return pl.pallas_call(
        timed,
        out_shape=out_shape,
        in_specs=[SMEM if i in smem else ANY if i in far else whole for i in range(n_in)] + [ANY] * after,
        scratch_shapes=list(scratch),
        out_specs=outs,
        compiler_params=pltpu.CompilerParams(vmem_limit_bytes=limit * 1024 * 1024),
        cost_estimate=pl.CostEstimate(flops=flops, bytes_accessed=moved, transcendentals=0),
    )


def shape(dims, dtype=BF):
    return jax.ShapeDtypeStruct(dims, dtype)


def nt(a, b):
    return lax.dot_general(a, b, (((1,), (1,)), ((), ())), preferred_element_type=F32)


def nn(a, b):
    return lax.dot_general(a, b, (((1,), (0,)), ((), ())), preferred_element_type=F32)


def iota(dims, axis):
    return lax.broadcasted_iota(jnp.int32, dims, axis)


def pick(target, rows=ROWS, first=0):
    span = target.shape[1]
    return (iota((rows, span), 0) + first == target).astype(F32).astype(BF)


def slots(onehots):
    total = sum(onehots)
    span = total.shape[1]
    before = (iota((span, span), 0) < iota((span, span), 1)).astype(F32).astype(BF)
    earlier = nn(total.astype(BF), before)
    return [jnp.sum(o * earlier, axis=0, keepdims=True).astype(jnp.int32) for o in onehots]


def place_body(experts, lengths, languages, enc, dec, sent, enc_at, dec_at):
    enc_count = enc.shape[1]
    dec_count = dec.shape[1]
    rank = iota((EXPERTS, enc_count), 0)
    named = [experts[k : k + 1, :] for k in range(2)]
    found = slots([(rank == e).astype(F32) for e in named])
    targets = [e * CAP + s for e, s in zip(named, found)]
    for k in range(2):
        enc_at[k : k + 1, :] = targets[k]

    sents = lengths.shape[1]
    square = (sents, sents)
    upto = iota(square, 1) <= iota(square, 0)
    same = iota(square, 1) == iota(square, 0)
    length = jnp.broadcast_to(lengths[...], square)
    language = jnp.broadcast_to(languages[...], square)
    ends = jnp.sum(jnp.where(upto, length, 0), axis=1, keepdims=True)
    begins = ends - jnp.sum(jnp.where(same, length, 0), axis=1, keepdims=True)
    spoken = jnp.sum(jnp.where(same, language, 0), axis=1, keepdims=True)
    places = iota((sents, dec_count), 1)
    member = (places >= begins) & (places < ends)
    chosen = jnp.sum(jnp.where(member, spoken, 0), axis=0, keepdims=True)
    dec_onehot = (iota((EXPERTS, dec_count), 0) == chosen).astype(F32)
    (dec_slot,) = slots([dec_onehot])
    dec_target = chosen * CAP + dec_slot
    dec_at[...] = dec_target

    zeros_enc = jnp.zeros((FEATS, enc_count), BF)
    zeros_dec = jnp.zeros((FEATS, dec_count), BF)
    wide_enc = jnp.concatenate([enc[...], zeros_enc], axis=0)
    wide_dec = jnp.concatenate([zeros_dec, dec[...]], axis=0)
    enc_pick = pick(targets[0]) + pick(targets[1])
    rows = nt(enc_pick, wide_enc) + nt(pick(dec_target), wide_dec)
    sent[:, :CAP, :] = rows.astype(BF).reshape(EXPERTS, CAP, 2 * FEATS)
    wide = (EXPERTS, 2 * FEATS)
    counts = jnp.broadcast_to(jnp.sum(dec_onehot, axis=1, keepdims=True), wide)
    on_lanes = jnp.sum(jnp.where(iota(wide, 0) == iota(wide, 1), counts, 0.0), axis=0, keepdims=True)
    for e in range(EXPERTS):
        line = iota((LINES - CAP, 2 * FEATS), 0)
        here = jnp.where(line == 0, on_lanes, jnp.where(line == 1, counts[e : e + 1], 0.0))
        sent[e, CAP:, :] = here.astype(BF)


def spread_body(got, enc, dec, rest, dec_at, most):
    turned = got[:, :CAP, :].reshape(ROWS, 2 * FEATS).astype(F32).T.astype(BF)
    tail = got[:, CAP:, :].astype(F32)
    totals = jnp.sum(tail[:, 0, :], axis=0, keepdims=True)
    most[0] = jnp.max(totals).astype(jnp.int32)
    counts = tail[:, 1, 0:1]
    group = iota((EXPERTS, ROWS), 1) // CAP
    own = jnp.sum(jnp.where(group == iota((EXPERTS, ROWS), 0), counts, 0.0), axis=0, keepdims=True)
    ahead = jnp.sum(jnp.where(group > iota((EXPERTS, ROWS), 0), counts, 0.0), axis=0, keepdims=True)
    slot = iota((1, ROWS), 1) % CAP
    at = jnp.where(slot < own.astype(jnp.int32), ahead.astype(jnp.int32) + slot, -1)
    dec_at[...] = at
    near = nt(turned[FEATS:], pick(at, HELD)).astype(BF)
    far = nt(turned[FEATS:], pick(at, ROWS - HELD, HELD)).astype(BF)
    dec[...] = near
    for t in range(T):
        enc[t] = turned[:FEATS]
        rest[t] = far


def turn_body(w_in, w_out, in_turned, out_turned, ready):
    ready[...] = jnp.zeros_like(ready)
    for d in range(DP):
        cut = [(t * DP + d) * FEATS for t in range(T)]
        block = jnp.concatenate([w_in[c : c + FEATS, :] for c in cut], axis=0)
        in_turned[d] = block.T
    for c in range(16):
        turned = w_out[:, c * 128 : (c + 1) * 128].T
        for half in range(2):
            b = c * 2 + half
            t, d = b // DP, b % DP
            out_turned[d, t * FEATS : (t + 1) * FEATS, :] = turned[half * FEATS : (half + 1) * FEATS]


def turn_near_body(me, w_in, w_out, in_turned, out_turned, ready):
    ready[...] = jnp.zeros_like(ready)
    span = DP * FEATS
    for t in range(T):
        for k in range(DP):
            at = pl.multiple_of((t * DP + lax.rem(me[0] - k + DP, DP)) * FEATS, FEATS)
            to = t * span + k * FEATS
            out_turned[to : to + FEATS, :] = w_in[pl.ds(at, FEATS), :]
    ordered = out_turned[...]
    in_turned[...] = ordered.T
    for t in range(T):
        block = w_out[:, t * span : (t + 1) * span].T
        for k in range(DP):
            to = pl.multiple_of(t * span + lax.rem(k - me[0] + DP, DP) * FEATS, FEATS)
            out_turned[pl.ds(to, FEATS), :] = block[k * FEATS : (k + 1) * FEATS]


def expert_body(me, x0, x1, x2, x3, w_in, w_out, p0, p1, p2, p3, xs, ins, outs, ps, sems):
    d = me[0]
    near = []
    for k, x in enumerate((x0, x1, x2, x3)):
        source = lax.rem(d - k + DP, DP)
        near.append(pltpu.make_async_copy(w_in.at[source], ins.at[k], sems.at[k]))
        near.append(pltpu.make_async_copy(x, xs.at[k], sems.at[DP + k]))
    far = {}
    for k in (2, 1, 3, 0):
        goal = lax.rem(d + k, DP)
        far[k] = pltpu.make_async_copy(w_out.at[goal], outs.at[k], sems.at[2 * DP + k])
    for copy in near + list(far.values()):
        copy.start()
    hidden = None
    for k in range(DP):
        near[2 * k].wait()
        near[2 * k + 1].wait()
        term = nn(ins[k], xs[k])
        hidden = term if hidden is None else hidden + term
    hidden = jnp.maximum(hidden, 0.0).astype(BF)
    gone = []
    for k in (2, 1, 3, 0):
        far[k].wait()
        ps[k] = nn(outs[k], hidden).astype(BF)
        gone.append(pltpu.make_async_copy(ps.at[k], (p0, p1, p2, p3)[k], sems.at[3 * DP + k]))
        gone[-1].start()
    for copy in gone:
        copy.wait()


def add_body(a, b, c, d, out):
    total = (a[...].astype(F32) + b[...].astype(F32)) + (c[...].astype(F32) + d[...].astype(F32))
    out[...] = total.astype(BF)


def total(ref):
    acc = ref[0].astype(F32)
    for t in range(1, T):
        acc = acc + ref[t].astype(F32)
    return acc.astype(BF)


def pack_body(enc, dec_a, dec_b, dec_c, dec_d, rest, dec_at, sent):
    at = dec_at[...]
    dec = sum(ref[...].astype(F32) for ref in (dec_a, dec_b, dec_c, dec_d)).astype(BF)
    back = nn(dec, pick(at, HELD)) + nn(total(rest), pick(at, ROWS - HELD, HELD))
    both = jnp.concatenate([total(enc).astype(F32), back], axis=0)
    sent[...] = both.T.astype(BF).reshape(EXPERTS, CAP, 2 * FEATS)


def mix_body(got, enc_at, dec_at, levels, enc, dec, enc_out, dec_out):
    turned = got[...].reshape(ROWS, 2 * FEATS).astype(F32).T.astype(BF)
    level = levels[...].astype(F32)
    whole = level[0:1] + level[1:2]
    mixed = enc[...].astype(F32)
    for k in range(2):
        rows = nn(turned[:FEATS], pick(enc_at[k : k + 1, :]))
        mixed = mixed + (level[k : k + 1] / whole) * rows
    enc_out[...] = mixed.astype(BF)
    rows = nn(turned[FEATS:], pick(dec_at[...]))
    dec_out[...] = (dec[...].astype(F32) + rows).astype(BF)


def shift(value, k):
    return lax.ppermute(value, "dp", [(i, (i + k) % DP) for i in range(DP)])


def over_tensor(block):
    return lax.all_to_all(block, "tensor", split_axis=0, concat_axis=0, tiled=True)


def gather(over_t):
    own = over_t.reshape(T * FEATS, over_t.shape[2])
    return [own] + [shift(own, k) for k in (1, 2, 3)]


def expert(blocks, turned, me):
    rows = blocks[0].shape[1]
    part = shape((T * FEATS, rows))
    work = 4 * rows * UNITS * T * DP * FEATS
    held = pltpu.VMEM((DP, T * FEATS, rows), BF)
    return call(
        expert_body,
        [part] * 4,
        7,
        smem=(0,),
        far=range(1, 7),
        far_out=True,
        scratch=[held, *(pltpu.VMEM(w.shape, BF) for w in turned), held, pltpu.SemaphoreType.DMA((4 * DP,))],
        limit=60,
        flops=work,
        moved=6 << 20,
    )(me, *blocks, *turned)


def arrive(parts):
    return [parts[0]] + [shift(parts[k], k) for k in (1, 2, 3)]


def settle(parts, later=()):
    rows = parts[0].shape[1]
    added = call(
        add_body, shape((T * FEATS, rows)), 4, moved=5 << 19, after=len(later)
    )(*parts, *later)
    return over_tensor(added.reshape(T, FEATS, rows))


def through(block, turned, me):
    return settle(arrive(expert(gather(over_tensor(block)), turned, me)))


def tie(values, others):
    done = lax.optimization_barrier((list(values), list(others)))
    return done[0], done[1]


def copies_body(a, b, c, d, out):
    for t in range(T):
        for k, ref in enumerate((a, b, c, d)):
            out[t, k] = ref[...]


def crossed_body(x, w_in, w_out, part, xs, ins, outs, ps, sems):
    span = T * FEATS
    first = pltpu.make_async_copy(w_in, ins, sems.at[0])
    near = []
    far = []
    for k in range(DP):
        cut = pl.ds(k * span, span)
        near.append(pltpu.make_async_copy(x.at[cut], xs.at[cut], sems.at[1 + k]))
        far.append(pltpu.make_async_copy(w_out.at[cut], outs.at[cut], sems.at[1 + DP + k]))
    for copy in [first] + near + far:
        copy.start()
    first.wait()
    hidden = None
    for k in range(DP):
        near[k].wait()
        term = nn(ins[:, k * span : (k + 1) * span], xs[k * span : (k + 1) * span, :])
        hidden = term if hidden is None else hidden + term
    hidden = jnp.maximum(hidden, 0.0).astype(BF)
    gone = []
    for k in range(DP):
        far[k].wait()
        cut = pl.ds(k * span, span)
        ps[k * span : (k + 1) * span, :] = nn(outs[k * span : (k + 1) * span, :], hidden).astype(BF)
        gone.append(pltpu.make_async_copy(ps.at[cut], part.at[cut], sems.at[1 + 2 * DP + k]))
        gone[-1].start()
    for copy in gone:
        copy.wait()


def crossed_sum_body(got, a, b, c, d):
    for k, ref in enumerate((a, b, c, d)):
        acc = got[0, k].astype(F32)
        for t in range(1, T):
            acc = acc + got[t, k].astype(F32)
        ref[...] = acc.astype(BF)


def expert_crossed(x, turned, later):
    rows = x.shape[3]
    flat = x.reshape(T * DP * FEATS, rows)
    work = 4 * rows * UNITS * T * DP * FEATS
    held = pltpu.VMEM(flat.shape, BF)
    part = call(
        crossed_body,
        shape(flat.shape),
        3,
        far=range(3),
        far_out=True,
        scratch=[held, *(pltpu.VMEM(w.shape, BF) for w in turned), held, pltpu.SemaphoreType.DMA((1 + 3 * DP,))],
        limit=60,
        flops=work,
        moved=4 << 20,
        after=len(later),
    )(flat, *turned, *later)
    return part.reshape(x.shape)


def shards(
    enc_tokens,
    enc_experts,
    enc_levels,
    enc_w_in,
    enc_w_out,
    dec_tokens,
    dec_lengths,
    dec_language,
    dec_w_in,
    dec_w_out,
):
    me = lax.axis_index("dp").astype(jnp.int32).reshape(1)
    enc = enc_tokens.T
    dec = dec_tokens.T
    packed = shape((EXPERTS, LINES, 2 * FEATS))
    sent, enc_at, dec_at = call(
        place_body,
        [packed, shape((2, enc.shape[1]), jnp.int32), shape((1, dec.shape[1]), jnp.int32)],
        5,
        limit=60,
        moved=1 << 18,
    )(enc_experts.T, dec_lengths, dec_language.T, enc, dec)
    got = lax.all_to_all(sent, "expert", split_axis=0, concat_axis=0, tiled=True)

    def turn(w_in, w_out):
        out = [shape((DP, UNITS, T * FEATS)), shape((DP, T * FEATS, UNITS)), shape((16, 128))]
        return call(turn_body, out, 2, limit=60, moved=4 << 20)(w_in[0], w_out[0])

    *enc_turned, enc_ready = turn(enc_w_in, enc_w_out)
    out = [shape((UNITS, T * DP * FEATS)), shape((T * DP * FEATS, UNITS)), shape((16, 128))]
    *near_turned, dec_ready = call(turn_near_body, out, 3, smem=(0,), limit=60, moved=4 << 20)(me, dec_w_in[0], dec_w_out[0])
    far = shape((T, FEATS, ROWS - HELD))
    enc_block, dec_block, rest_block, moved_to, most = call(
        spread_body,
        [shape((T, FEATS, ROWS)), shape((FEATS, HELD)), far, shape((1, ROWS), jnp.int32), shape((1,), jnp.int32)],
        1,
        smem_out=(4,),
        moved=1 << 20,
    )(got)

    near_x = [dec_block] + [shift(dec_block, k) for k in (1, 2, 3)]
    dec_x = call(copies_body, shape((T, DP, FEATS, HELD)), 4, moved=1 << 20, after=2)(
        *near_x, enc_ready, dec_ready
    )
    enc_t = over_tensor(enc_block)
    (dec_x,), (enc_t,) = tie([dec_x], [enc_t])
    enc_x = gather(enc_t)
    dec_x = over_tensor(dec_x)
    dec_parts = expert_crossed(dec_x, near_turned, enc_x[1:])
    enc_got = arrive(expert(enc_x, enc_turned, me))
    dec_parts = over_tensor(dec_parts)
    dec_halves = call(crossed_sum_body, [shape((FEATS, HELD))] * 4, 1, moved=1 << 20)(dec_parts)
    dec_sums = arrive(dec_halves)
    enc_sums = settle(enc_got, [dec_parts])
    rest_sums = lax.cond(
        most[0] > HELD,
        lambda b, w: through(b, turn(*w)[:2], me),
        lambda b, w: jnp.zeros_like(b),
        rest_block,
        (dec_w_in, dec_w_out),
    )

    packed = shape((EXPERTS, CAP, 2 * FEATS))
    back = call(pack_body, packed, 7, moved=1 << 20)(enc_sums, *dec_sums, rest_sums, moved_to)
    got = lax.all_to_all(back, "expert", split_axis=0, concat_axis=0, tiled=True)
    enc_out, dec_out = call(
        mix_body, [shape(enc.shape), shape(dec.shape)], 6, moved=1 << 18
    )(got, enc_at, dec_at, enc_levels.T, enc, dec)
    return enc_out.T, dec_out.T


def solution(mesh):
    return jax.shard_map(
        shards,
        mesh=mesh,
        in_specs=(
            P("expert", ("tensor", "dp")),
            P("expert", None),
            P("expert", None),
            P("expert", None, ("tensor", "dp")),
            P("expert", ("tensor", "dp"), None),
            P("expert", ("tensor", "dp")),
            P("expert", None),
            P("expert", None),
            P("expert", None, ("tensor", "dp")),
            P("expert", ("tensor", "dp"), None),
        ),
        out_specs=(P("expert", ("tensor", "dp")), P("expert", ("tensor", "dp"))),
        check_vma=False,
    )
```

```python
import jax
import jax.numpy as jnp
from jax import lax
from jax.experimental import pallas as pl
from jax.experimental.pallas import tpu as pltpu
from jax.sharding import PartitionSpec as P

BF = jnp.bfloat16
F32 = jnp.float32
EXPERTS = 16
CAP = 32
ROWS = EXPERTS * CAP
FEATS = 64
HELD = 256
LINES = CAP + 16
T = 8
DP = 4
UNITS = 256
VMEM = pl.BlockSpec(memory_space=pltpu.VMEM)
SMEM = pl.BlockSpec(memory_space=pltpu.SMEM)
ANY = pl.BlockSpec(memory_space=pl.ANY)


def call(body, out_shape, n_in, *, smem=(), smem_out=(), limit=32, flops=0, moved=0, after=0, far=(), far_out=False, scratch=()):
    def timed(*refs):
        body(*refs[:n_in], *refs[n_in + after :])

    many = isinstance(out_shape, (tuple, list))
    whole = pl.BlockSpec() if limit > 32 else VMEM
    place = ANY if far_out else whole
    outs = [SMEM if i in smem_out else place for i in range(len(out_shape))] if many else place
    return pl.pallas_call(
        timed,
        out_shape=out_shape,
        in_specs=[SMEM if i in smem else ANY if i in far else whole for i in range(n_in)] + [ANY] * after,
        scratch_shapes=list(scratch),
        out_specs=outs,
        compiler_params=pltpu.CompilerParams(vmem_limit_bytes=limit * 1024 * 1024),
        cost_estimate=pl.CostEstimate(flops=flops, bytes_accessed=moved, transcendentals=0),
    )


def shape(dims, dtype=BF):
    return jax.ShapeDtypeStruct(dims, dtype)


def nt(a, b):
    return lax.dot_general(a, b, (((1,), (1,)), ((), ())), preferred_element_type=F32)


def nn(a, b):
    return lax.dot_general(a, b, (((1,), (0,)), ((), ())), preferred_element_type=F32)


def iota(dims, axis):
    return lax.broadcasted_iota(jnp.int32, dims, axis)


def pick(target, rows=ROWS, first=0):
    span = target.shape[1]
    return (iota((rows, span), 0) + first == target).astype(F32).astype(BF)


def slots(onehots):
    total = sum(onehots)
    span = total.shape[1]
    before = (iota((span, span), 0) < iota((span, span), 1)).astype(F32).astype(BF)
    earlier = nn(total.astype(BF), before)
    return [jnp.sum(o * earlier, axis=0, keepdims=True).astype(jnp.int32) for o in onehots]


def place_body(experts, lengths, languages, enc, dec, sent, enc_at, dec_at):
    enc_count = enc.shape[1]
    dec_count = dec.shape[1]
    rank = iota((EXPERTS, enc_count), 0)
    named = [experts[k : k + 1, :] for k in range(2)]
    found = slots([(rank == e).astype(F32) for e in named])
    targets = [e * CAP + s for e, s in zip(named, found)]
    for k in range(2):
        enc_at[k : k + 1, :] = targets[k]

    sents = lengths.shape[1]
    square = (sents, sents)
    upto = iota(square, 1) <= iota(square, 0)
    same = iota(square, 1) == iota(square, 0)
    length = jnp.broadcast_to(lengths[...], square)
    language = jnp.broadcast_to(languages[...], square)
    ends = jnp.sum(jnp.where(upto, length, 0), axis=1, keepdims=True)
    begins = ends - jnp.sum(jnp.where(same, length, 0), axis=1, keepdims=True)
    spoken = jnp.sum(jnp.where(same, language, 0), axis=1, keepdims=True)
    places = iota((sents, dec_count), 1)
    member = (places >= begins) & (places < ends)
    chosen = jnp.sum(jnp.where(member, spoken, 0), axis=0, keepdims=True)
    dec_onehot = (iota((EXPERTS, dec_count), 0) == chosen).astype(F32)
    (dec_slot,) = slots([dec_onehot])
    dec_target = chosen * CAP + dec_slot
    dec_at[...] = dec_target

    zeros_enc = jnp.zeros((FEATS, enc_count), BF)
    zeros_dec = jnp.zeros((FEATS, dec_count), BF)
    wide_enc = jnp.concatenate([enc[...], zeros_enc], axis=0)
    wide_dec = jnp.concatenate([zeros_dec, dec[...]], axis=0)
    enc_pick = pick(targets[0]) + pick(targets[1])
    rows = nt(enc_pick, wide_enc) + nt(pick(dec_target), wide_dec)
    sent[:, :CAP, :] = rows.astype(BF).reshape(EXPERTS, CAP, 2 * FEATS)
    wide = (EXPERTS, 2 * FEATS)
    counts = jnp.broadcast_to(jnp.sum(dec_onehot, axis=1, keepdims=True), wide)
    on_lanes = jnp.sum(jnp.where(iota(wide, 0) == iota(wide, 1), counts, 0.0), axis=0, keepdims=True)
    for e in range(EXPERTS):
        line = iota((LINES - CAP, 2 * FEATS), 0)
        here = jnp.where(line == 0, on_lanes, jnp.where(line == 1, counts[e : e + 1], 0.0))
        sent[e, CAP:, :] = here.astype(BF)


def spread_body(got, enc, dec, rest, dec_at, most):
    turned = got[:, :CAP, :].reshape(ROWS, 2 * FEATS).astype(F32).T.astype(BF)
    tail = got[:, CAP:, :].astype(F32)
    totals = jnp.sum(tail[:, 0, :], axis=0, keepdims=True)
    most[0] = jnp.max(totals).astype(jnp.int32)
    counts = tail[:, 1, 0:1]
    group = iota((EXPERTS, ROWS), 1) // CAP
    own = jnp.sum(jnp.where(group == iota((EXPERTS, ROWS), 0), counts, 0.0), axis=0, keepdims=True)
    ahead = jnp.sum(jnp.where(group > iota((EXPERTS, ROWS), 0), counts, 0.0), axis=0, keepdims=True)
    slot = iota((1, ROWS), 1) % CAP
    at = jnp.where(slot < own.astype(jnp.int32), ahead.astype(jnp.int32) + slot, -1)
    dec_at[...] = at
    near = nt(turned[FEATS:], pick(at, HELD)).astype(BF)
    far = nt(turned[FEATS:], pick(at, ROWS - HELD, HELD)).astype(BF)
    dec[...] = near
    for t in range(T):
        enc[t] = turned[:FEATS]
        rest[t] = far


def turn_body(w_in, w_out, in_turned, out_turned, ready):
    ready[...] = jnp.zeros_like(ready)
    for d in range(DP):
        cut = [(t * DP + d) * FEATS for t in range(T)]
        block = jnp.concatenate([w_in[c : c + FEATS, :] for c in cut], axis=0)
        in_turned[d] = block.T
    for c in range(16):
        turned = w_out[:, c * 128 : (c + 1) * 128].T
        for half in range(2):
            b = c * 2 + half
            t, d = b // DP, b % DP
            out_turned[d, t * FEATS : (t + 1) * FEATS, :] = turned[half * FEATS : (half + 1) * FEATS]


def turn_near_body(me, w_in, w_out, in_turned, out_turned, ready):
    ready[...] = jnp.zeros_like(ready)
    span = DP * FEATS
    for t in range(T):
        for k in range(DP):
            at = pl.multiple_of((t * DP + lax.rem(me[0] - k + DP, DP)) * FEATS, FEATS)
            to = t * span + k * FEATS
            out_turned[to : to + FEATS, :] = w_in[pl.ds(at, FEATS), :]
    ordered = out_turned[...]
    in_turned[...] = ordered.T
    for t in range(T):
        block = w_out[:, t * span : (t + 1) * span].T
        for k in range(DP):
            to = pl.multiple_of(t * span + lax.rem(k - me[0] + DP, DP) * FEATS, FEATS)
            out_turned[pl.ds(to, FEATS), :] = block[k * FEATS : (k + 1) * FEATS]


def expert_steps(me, x0, x1, x2, x3, w_in, w_out, p0, p1, p2, p3, xs, ins, outs, ps, sems):
    d = me[0]
    near = []
    for k, x in enumerate((x0, x1, x2, x3)):
        source = lax.rem(d - k + DP, DP)
        near.append(pltpu.make_async_copy(w_in.at[source], ins.at[k], sems.at[k]))
        near.append(pltpu.make_async_copy(x, xs.at[k], sems.at[DP + k]))
    far = {}
    for k in (2, 1, 3, 0):
        goal = lax.rem(d + k, DP)
        far[k] = pltpu.make_async_copy(w_out.at[goal], outs.at[k], sems.at[2 * DP + k])
    for copy in near + list(far.values()):
        copy.start()
    yield
    hidden = None
    for k in range(DP):
        near[2 * k].wait()
        near[2 * k + 1].wait()
        term = nn(ins[k], xs[k])
        hidden = term if hidden is None else hidden + term
    hidden = jnp.maximum(hidden, 0.0).astype(BF)
    gone = []
    for k in (2, 1, 3, 0):
        far[k].wait()
        ps[k] = nn(outs[k], hidden).astype(BF)
        gone.append(pltpu.make_async_copy(ps.at[k], (p0, p1, p2, p3)[k], sems.at[3 * DP + k]))
        gone[-1].start()
    yield
    for copy in gone:
        copy.wait()


def expert_body(*refs):
    for _ in expert_steps(*refs):
        pass


def both_body(me, x0, x1, x2, x3, e_in, e_out, x, d_in, d_out, p0, p1, p2, p3, part, *held):
    near = crossed_steps(x, d_in, d_out, part, *held[5:])
    far = expert_steps(me, x0, x1, x2, x3, e_in, e_out, p0, p1, p2, p3, *held[:5])
    for _ in zip(near, far):
        pass
    next(far, None)


def add_body(a, b, c, d, out):
    total = (a[...].astype(F32) + b[...].astype(F32)) + (c[...].astype(F32) + d[...].astype(F32))
    out[...] = total.astype(BF)


def total(ref):
    acc = ref[0].astype(F32)
    for t in range(1, T):
        acc = acc + ref[t].astype(F32)
    return acc.astype(BF)


def pack_body(enc, dec_a, dec_b, dec_c, dec_d, rest, dec_at, sent):
    at = dec_at[...]
    dec = sum(ref[...].astype(F32) for ref in (dec_a, dec_b, dec_c, dec_d)).astype(BF)
    back = nn(dec, pick(at, HELD)) + nn(total(rest), pick(at, ROWS - HELD, HELD))
    both = jnp.concatenate([total(enc).astype(F32), back], axis=0)
    sent[...] = both.T.astype(BF).reshape(EXPERTS, CAP, 2 * FEATS)


def mix_body(got, enc_at, dec_at, levels, enc, dec, enc_out, dec_out):
    turned = got[...].reshape(ROWS, 2 * FEATS).astype(F32).T.astype(BF)
    level = levels[...].astype(F32)
    whole = level[0:1] + level[1:2]
    mixed = enc[...].astype(F32)
    for k in range(2):
        rows = nn(turned[:FEATS], pick(enc_at[k : k + 1, :]))
        mixed = mixed + (level[k : k + 1] / whole) * rows
    enc_out[...] = mixed.astype(BF)
    rows = nn(turned[FEATS:], pick(dec_at[...]))
    dec_out[...] = (dec[...].astype(F32) + rows).astype(BF)


def shift(value, k):
    return lax.ppermute(value, "dp", [(i, (i + k) % DP) for i in range(DP)])


def over_tensor(block):
    return lax.all_to_all(block, "tensor", split_axis=0, concat_axis=0, tiled=True)


def gather(over_t):
    own = over_t.reshape(T * FEATS, over_t.shape[2])
    return [own] + [shift(own, k) for k in (1, 2, 3)]


def held_for(rows, turned, sems):
    held = pltpu.VMEM((DP, T * FEATS, rows), BF)
    return [held, *(pltpu.VMEM(w.shape, BF) for w in turned), held, pltpu.SemaphoreType.DMA((sems,))]


def expert(blocks, turned, me):
    rows = blocks[0].shape[1]
    part = shape((T * FEATS, rows))
    return call(
        expert_body,
        [part] * 4,
        7,
        smem=(0,),
        far=range(1, 7),
        far_out=True,
        scratch=held_for(rows, turned, 4 * DP),
        limit=60,
        flops=4 * rows * UNITS * T * DP * FEATS,
        moved=6 << 20,
    )(me, *blocks, *turned)


def both_experts(blocks, turned, x, near_turned, me):
    rows, near_rows = blocks[0].shape[1], x.shape[3]
    flat = x.reshape(T * DP * FEATS, near_rows)
    near = [pltpu.VMEM(flat.shape, BF), *(pltpu.VMEM(w.shape, BF) for w in near_turned)]
    *parts, part = call(
        both_body,
        [shape((T * FEATS, rows))] * 4 + [shape(flat.shape)],
        10,
        smem=(0,),
        far=range(1, 10),
        far_out=True,
        scratch=held_for(rows, turned, 4 * DP)
        + near
        + [pltpu.VMEM(flat.shape, BF), pltpu.SemaphoreType.DMA((1 + 3 * DP,))],
        limit=60,
        flops=4 * (rows + near_rows) * UNITS * T * DP * FEATS,
        moved=10 << 20,
    )(me, *blocks, *turned, flat, *near_turned)
    return parts, part.reshape(x.shape)


def arrive(parts):
    return [parts[0]] + [shift(parts[k], k) for k in (1, 2, 3)]


def settle(parts, later=()):
    rows = parts[0].shape[1]
    added = call(
        add_body, shape((T * FEATS, rows)), 4, moved=5 << 19, after=len(later)
    )(*parts, *later)
    return over_tensor(added.reshape(T, FEATS, rows))


def through(block, turned, me):
    return settle(arrive(expert(gather(over_tensor(block)), turned, me)))


def tie(values, others):
    done = lax.optimization_barrier((list(values), list(others)))
    return done[0], done[1]


def copies_body(a, b, c, d, out):
    for t in range(T):
        for k, ref in enumerate((a, b, c, d)):
            out[t, k] = ref[...]


def crossed_steps(x, w_in, w_out, part, xs, ins, outs, ps, sems):
    span = T * FEATS
    first = pltpu.make_async_copy(w_in, ins, sems.at[0])
    near = []
    far = []
    for k in range(DP):
        cut = pl.ds(k * span, span)
        near.append(pltpu.make_async_copy(x.at[cut], xs.at[cut], sems.at[1 + k]))
        far.append(pltpu.make_async_copy(w_out.at[cut], outs.at[cut], sems.at[1 + DP + k]))
    for copy in [first] + near + far:
        copy.start()
    yield
    first.wait()
    hidden = None
    for k in range(DP):
        near[k].wait()
        term = nn(ins[:, k * span : (k + 1) * span], xs[k * span : (k + 1) * span, :])
        hidden = term if hidden is None else hidden + term
    hidden = jnp.maximum(hidden, 0.0).astype(BF)
    gone = []
    for k in range(DP):
        far[k].wait()
        cut = pl.ds(k * span, span)
        ps[k * span : (k + 1) * span, :] = nn(outs[k * span : (k + 1) * span, :], hidden).astype(BF)
        gone.append(pltpu.make_async_copy(ps.at[cut], part.at[cut], sems.at[1 + 2 * DP + k]))
        gone[-1].start()
    yield
    for copy in gone:
        copy.wait()


def crossed_sum_body(got, a, b, c, d):
    for k, ref in enumerate((a, b, c, d)):
        acc = got[0, k].astype(F32)
        for t in range(1, T):
            acc = acc + got[t, k].astype(F32)
        ref[...] = acc.astype(BF)


def shards(
    enc_tokens,
    enc_experts,
    enc_levels,
    enc_w_in,
    enc_w_out,
    dec_tokens,
    dec_lengths,
    dec_language,
    dec_w_in,
    dec_w_out,
):
    me = lax.axis_index("dp").astype(jnp.int32).reshape(1)
    enc = enc_tokens.T
    dec = dec_tokens.T
    packed = shape((EXPERTS, LINES, 2 * FEATS))
    sent, enc_at, dec_at = call(
        place_body,
        [packed, shape((2, enc.shape[1]), jnp.int32), shape((1, dec.shape[1]), jnp.int32)],
        5,
        limit=60,
        moved=1 << 18,
    )(enc_experts.T, dec_lengths, dec_language.T, enc, dec)
    got = lax.all_to_all(sent, "expert", split_axis=0, concat_axis=0, tiled=True)

    def turn(w_in, w_out):
        out = [shape((DP, UNITS, T * FEATS)), shape((DP, T * FEATS, UNITS)), shape((16, 128))]
        return call(turn_body, out, 2, limit=60, moved=4 << 20)(w_in[0], w_out[0])

    *enc_turned, enc_ready = turn(enc_w_in, enc_w_out)
    out = [shape((UNITS, T * DP * FEATS)), shape((T * DP * FEATS, UNITS)), shape((16, 128))]
    *near_turned, dec_ready = call(turn_near_body, out, 3, smem=(0,), limit=60, moved=4 << 20)(me, dec_w_in[0], dec_w_out[0])
    far = shape((T, FEATS, ROWS - HELD))
    enc_block, dec_block, rest_block, moved_to, most = call(
        spread_body,
        [shape((T, FEATS, ROWS)), shape((FEATS, HELD)), far, shape((1, ROWS), jnp.int32), shape((1,), jnp.int32)],
        1,
        smem_out=(4,),
        moved=1 << 20,
        after=1,
    )(got, enc_ready)

    near_x = [dec_block] + [shift(dec_block, k) for k in (1, 2, 3)]
    dec_x = call(copies_body, shape((T, DP, FEATS, HELD)), 4, moved=1 << 20)(*near_x)
    enc_t = over_tensor(enc_block)
    (dec_x,), (enc_t,) = tie([dec_x], [enc_t])
    enc_x = gather(enc_t)
    dec_x = over_tensor(dec_x)
    enc_parts, dec_parts = both_experts(enc_x, enc_turned, dec_x, near_turned, me)
    enc_got = arrive(enc_parts)
    dec_parts = over_tensor(dec_parts)
    dec_halves = call(crossed_sum_body, [shape((FEATS, HELD))] * 4, 1, moved=1 << 20)(dec_parts)
    dec_sums = arrive(dec_halves)
    enc_sums = settle(enc_got, [dec_parts])
    rest_sums = lax.cond(
        most[0] > HELD,
        lambda b, w: through(b, turn(*w)[:2], me),
        lambda b, w: jnp.zeros_like(b),
        rest_block,
        (dec_w_in, dec_w_out),
    )

    packed = shape((EXPERTS, CAP, 2 * FEATS))
    back = call(pack_body, packed, 7, moved=1 << 20)(enc_sums, *dec_sums, rest_sums, moved_to)
    got = lax.all_to_all(back, "expert", split_axis=0, concat_axis=0, tiled=True)
    enc_out, dec_out = call(
        mix_body, [shape(enc.shape), shape(dec.shape)], 6, moved=1 << 18
    )(got, enc_at, dec_at, enc_levels.T, enc, dec)
    return enc_out.T, dec_out.T


def solution(mesh):
    return jax.shard_map(
        shards,
        mesh=mesh,
        in_specs=(
            P("expert", ("tensor", "dp")),
            P("expert", None),
            P("expert", None),
            P("expert", None, ("tensor", "dp")),
            P("expert", ("tensor", "dp"), None),
            P("expert", ("tensor", "dp")),
            P("expert", None),
            P("expert", None),
            P("expert", None, ("tensor", "dp")),
            P("expert", ("tensor", "dp"), None),
        ),
        out_specs=(P("expert", ("tensor", "dp")), P("expert", ("tensor", "dp"))),
        check_vma=False,
    )
```
